256 devices in a mesh: dp: 8 (over y, x_hi), space: 32 (over x_lo, z, core).
Axes of the slice: x: 4 (x_hi: 2, x_lo: 2; x = x_hi * 2 + x_lo), y: 4, z: 8, core: 2. Of those that a mesh axis runs over, the one named last changes fastest.
Arguments:
- field: bfloat16 [8, 64, 1024, 1024], P('dp', None, 'space'), may hold values from -6 to 6
- cotangent: bfloat16 [8, 64, 1024, 1024], P('dp', None, 'space'), may hold values from -6 to 6
- spectral_weight: bfloat16 [64, 64, 64, 128], P('dp', 'space'), may hold values from -4 to 4
- mixing_weight: bfloat16 [64, 64], replicated, may hold values from -0.75 to 0.75
- bias: float32 [64], replicated, may hold values from -3 to 3
Outputs:
- field_grad: bfloat16 [8, 64, 1024, 1024], P('dp', None, 'space')
- spectral_grad: float32 [64, 64, 64, 128], P('dp', 'space')
- mixing_grad: float32 [64, 64], replicated
- bias_grad: float32 [64], replicated
The draws below stay inside these ranges and needn't reach their ends.
All inputs are finite; a program needn't handle non-finite values.
Results may differ from the reference program's by a relative error of at most 0.02.
Values may be sent and summed in bfloat16 or wider, within the bound.
A program may use at most 128 MiB of HBM per device.

```python
import math
import jax
import jax.numpy as jnp
from jax import lax

C = 64
H = 1024
W = 1024
K1 = 64
K2 = 64
B = 8


def block_scale(key, extent, cuts, low, high):
    level = 1.0
    for dim, parts in cuts:
        steps = jax.random.uniform(jax.random.fold_in(jax.random.fold_in(key, 6), dim), (parts,), jnp.float32, low / len(cuts), high / len(cuts))
        level = level * jnp.repeat(jnp.exp(steps), extent[dim] // parts).reshape((-1,) + (1,) * (len(extent) - 1 - dim))
    return level


def bell_draw(stream_key, dims, scale, bound, cuts=(), kind=jnp.bfloat16):
    level = block_scale(stream_key, dims, cuts, -0.22, 0.18) if cuts else 1.0
    values = jax.random.normal(stream_key, dims, jnp.float32) * scale * level
    return jnp.minimum(jnp.maximum(values, -bound), bound).astype(kind)


def setup_inputs(seed: int = 0) -> dict:
    streams_of = jax.random.split(jax.random.key(seed), 6)
    field = bell_draw(streams_of[0], (B, C, H, W), 1.0, 6.0, ((0, 8), (2, 32)))
    cotangent = bell_draw(streams_of[1], (B, C, H, W), 1.0, 6.0, ((0, 8), (2, 32)))
    spectral_weight = bell_draw(streams_of[2], (K1, K2, C, 2 * C), (max(C // 32, 1)) ** -0.5, 4.0, ((0, 8), (1, 32)))
    mixing_weight = bell_draw(streams_of[3], (C, C), C ** -0.5, 0.75)
    bias = bell_draw(streams_of[4], (C,), 0.5, 3.0, (), jnp.float32)
    return dict(field=field, cotangent=cotangent, spectral_weight=spectral_weight, mixing_weight=mixing_weight, bias=bias)


HIGH = lax.Precision.HIGHEST

def build_tables():
    wpos = jnp.arange(W, dtype=jnp.int32)[:, None]
    kpos = jnp.arange(K2, dtype=jnp.int32)[None, :]
    angle = (wpos * kpos % W).astype(jnp.float32) * (2.0 * math.pi / W)
    scale = 1.0 / math.sqrt(W)
    cosine = jnp.cos(angle) * scale
    sine = jnp.sin(angle) * scale
    colfwd = jnp.stack([cosine, -sine], -1).reshape(W, 2 * K2).astype(jnp.bfloat16)
    factor = jnp.where(kpos == 0, 1.0, 2.0).astype(jnp.float32)
    colinv = jnp.stack([factor * cosine, -factor * sine], -1).reshape(W, 2 * K2).T.astype(jnp.bfloat16)
    mpos = jnp.arange(K1, dtype=jnp.int32)[:, None]
    freq = mpos + jnp.where(mpos >= K1 // 2, H - K1, 0).astype(jnp.int32)
    hpos = jnp.arange(H, dtype=jnp.int32)[None, :]
    phase = (freq * hpos % H).astype(jnp.float32) * (2.0 * math.pi / H)
    row_cosine_table = (jnp.cos(phase) / math.sqrt(H)).astype(jnp.bfloat16)
    row_sine_table = (jnp.sin(phase) / math.sqrt(H)).astype(jnp.bfloat16)
    return (colfwd, colinv, row_cosine_table, row_sine_table)

def weave(real_part, imag_part):
    return jnp.stack([real_part, imag_part], -1).reshape(real_part.shape[:-1] + (2 * real_part.shape[-1],))

def frequency_total(form, left, right):
    return jnp.einsum(form, left.astype(jnp.float32), right.astype(jnp.float32), precision=HIGH)

def row_forward(value_entries, row_cosine_table, row_sine_table):
    value_real, value_imaginary = (value_entries[..., 0::2], value_entries[..., 1::2])
    output_real = frequency_total('ye,fwei->fwyi', row_cosine_table, value_real) + frequency_total('ye,fwei->fwyi', row_sine_table, value_imaginary)
    output_imaginary = frequency_total('ye,fwei->fwyi', row_cosine_table, value_imaginary) - frequency_total('ye,fwei->fwyi', row_sine_table, value_real)
    return weave(output_real, output_imaginary)

def row_inverse(value_entries, row_cosine_table, row_sine_table):
    value_real, value_imaginary = (value_entries[..., 0::2], value_entries[..., 1::2])
    output_real = frequency_total('xu,qwxy->qwuy', row_cosine_table, value_real) - frequency_total('xu,qwxy->qwuy', row_sine_table, value_imaginary)
    output_imaginary = frequency_total('xu,qwxy->qwuy', row_cosine_table, value_imaginary) + frequency_total('xu,qwxy->qwuy', row_sine_table, value_real)
    return weave(output_real, output_imaginary)

def reference(field, cotangent, spectral_weight, mixing_weight, bias):
    colfwd, colinv, row_cosine_table, row_sine_table = build_tables()
    wre, wim = (spectral_weight[..., :C], spectral_weight[..., C:])

    def first_section(sample):
        colmodes = frequency_total('chw,wk->chk', sample, colfwd).astype(jnp.bfloat16)
        return row_forward(colmodes[None], row_cosine_table, row_sine_table)[0].astype(jnp.bfloat16)
    modes = lax.map(first_section, field)
    xre, xim = (modes[..., 0::2], modes[..., 1::2])
    mix_re = frequency_total('bimk,mkio->bomk', xre, wre) - frequency_total('bimk,mkio->bomk', xim, wim)
    mix_im = frequency_total('bimk,mkio->bomk', xre, wim) + frequency_total('bimk,mkio->bomk', xim, wre)
    mixed = weave(mix_re, mix_im).astype(jnp.bfloat16)

    def second_section(items):
        mixed_one, sample, cot_one = items
        rowback = row_inverse(mixed_one[None], row_cosine_table, row_sine_table)[0].astype(jnp.bfloat16)
        pre = frequency_total('chk,kw->chw', rowback, colinv) + frequency_total('ihw,io->ohw', sample, mixing_weight) + bias[:, None, None]
        gelu_out, pull = jax.vjp(jax.nn.gelu, pre)
        pregrad = pull(cot_one.astype(pre.dtype))[0].astype(jnp.bfloat16)
        weight_part = frequency_total('ihw,ohw->io', sample, pregrad)
        bias_part = lax.optimization_barrier(jnp.sum(pregrad.astype(jnp.float32), axis=(1, 2)))
        colgrad = frequency_total('ohw,kw->ohk', pregrad, colinv).astype(jnp.bfloat16)
        modegrad = row_forward(colgrad[None], row_cosine_table, row_sine_table)[0].astype(jnp.bfloat16)
        return (modegrad, pregrad, weight_part, bias_part)
    modegrad, pregrad, weight_parts, bias_parts = lax.map(second_section, (mixed, field, cotangent))
    norm = 1.0 / math.sqrt(B * H * W)
    mixing_grad = lax.optimization_barrier(jnp.sum(weight_parts, axis=0)) * norm
    bias_grad = lax.optimization_barrier(jnp.sum(bias_parts, axis=0)) * norm
    gre, gim = (modegrad[..., 0::2], modegrad[..., 1::2])
    grad_re = frequency_total('bimk,bomk->mkio', xre, gre) + frequency_total('bimk,bomk->mkio', xim, gim)
    grad_im = frequency_total('bimk,bomk->mkio', xre, gim) - frequency_total('bimk,bomk->mkio', xim, gre)
    spectral_grad = jnp.concatenate([grad_re, grad_im], axis=-1)
    in_re = frequency_total('bomk,mkio->bimk', gre, wre) + frequency_total('bomk,mkio->bimk', gim, wim)
    in_im = frequency_total('bomk,mkio->bimk', gim, wre) - frequency_total('bomk,mkio->bimk', gre, wim)
    inputgrad = weave(in_re, in_im).astype(jnp.bfloat16)

    def third_section(items):
        grad_one, pre_one = items
        rowgrad = row_inverse(grad_one[None], row_cosine_table, row_sine_table)[0].astype(jnp.bfloat16)
        total = frequency_total('ihk,wk->ihw', rowgrad, colfwd) + frequency_total('ohw,io->ihw', pre_one, mixing_weight)
        return total.astype(jnp.bfloat16)
    field_grad = lax.map(third_section, (inputgrad, pregrad))
    return (field_grad, spectral_grad, mixing_grad, bias_grad)
```

```python
import functools
import math

import jax
import jax.numpy as jnp
import ml_dtypes
import numpy as np
from jax import lax
from jax.experimental import pallas as pl
from jax.experimental.pallas import tpu as pltpu
from jax.sharding import PartitionSpec as P

C = 64
H = 1024
W = 1024
K1 = 64
K2 = 64
DP = 8
NZ = 8
NQ = 4
SLAB = 32
BF = jnp.bfloat16
F32 = jnp.float32
NN = (((1,), (0,)), ((), ()))
NT = (((1,), (1,)), ((), ()))


def build_tables():
    f32 = np.float32
    wpos = np.arange(W)[:, None]
    kpos = np.arange(K2)[None, :]
    angle = (wpos * kpos % W).astype(f32) * f32(2.0 * math.pi / W)
    scale = f32(1.0 / math.sqrt(W))
    cosine = np.cos(angle) * scale
    sine = np.sin(angle) * scale
    factor = np.where(kpos == 0, 1.0, 2.0).astype(f32)
    fwd = np.stack([cosine, -sine], 0).astype(ml_dtypes.bfloat16)
    inv = np.stack([factor * cosine, -factor * sine], 0).astype(ml_dtypes.bfloat16)
    z, xl, core, kk = np.meshgrid(
        np.arange(NZ), np.arange(2), np.arange(2), np.arange(2), indexing="ij"
    )
    order = (2 * (xl * 16 + z * 2 + core) + kk).reshape(-1)
    colfwd = fwd[:, :, order].transpose(1, 2, 0).reshape(W, 2 * K2)
    colinv_t = inv[:, :, order].transpose(1, 2, 0).reshape(W, 2 * K2)
    colinv = inv[:, :, order].transpose(0, 2, 1).reshape(2 * K2, W)
    colfwd_t = fwd[:, :, order].transpose(0, 2, 1).reshape(2 * K2, W)

    mpos = np.arange(K1)[:, None]
    freq = mpos + np.where(mpos >= K1 // 2, H - K1, 0)
    hpos = np.arange(H)[None, :]
    phase = (freq * hpos % H).astype(f32) * f32(2.0 * math.pi / H)
    rc = (np.cos(phase) / f32(math.sqrt(H))).astype(ml_dtypes.bfloat16)
    rs = (np.sin(phase) / f32(math.sqrt(H))).astype(ml_dtypes.bfloat16)
    fwd_rows = []
    inv_rows = []
    for zi in range(NZ):
        slabs = np.array([x * 16 + zi * 2 + c for x in range(2) for c in range(2)])
        rows = slabs[:, None, None] * SLAB + np.arange(16)[None, :, None] * 2 + np.arange(2)
        ct = rc[:, rows].reshape(DP, 8, NQ, 16, 2)
        st = rs[:, rows].reshape(DP, 8, NQ, 16, 2)
        big = np.zeros((2, 2, DP, 2, 8, NQ, 2, 2, 16), ml_dtypes.bfloat16)
        for hl in range(2):
            for k in range(2):
                big[hl, 0, :, k, :, :, k, 0] = ct[..., hl]
                big[hl, 0, :, k, :, :, k, 1] = st[..., hl]
                big[hl, 1, :, k, :, :, k, 0] = -st[..., hl]
                big[hl, 1, :, k, :, :, k, 1] = ct[..., hl]
        fwd_rows.append(big.reshape(512, 256))
        rows = slabs[:, None] * SLAB + np.arange(SLAB)[None, :]
        tab = np.zeros((2, NQ, 2, SLAB, DP, 2, 8), ml_dtypes.bfloat16)
        for i, t in enumerate((rc, rs)):
            v = t[:, rows].reshape(DP, 8, NQ, SLAB).transpose(2, 3, 0, 1)
            for k in range(2):
                tab[i, :, k, :, :, k, :] = v
        inv_rows.append(tab.reshape(512, 128))
    return colfwd, colinv_t, colinv, colfwd_t, np.stack(fwd_rows), np.stack(inv_rows)


def far_first(i):
    step = (i + 1) // 2
    return lax.rem(4 + step * (2 * lax.rem(i, 2) - 1) + 8, 8)


def kernel(
    field_h, cot_h, sw_h, colfwd_h, colinvt_h, colinv_h, colfwdt_h, rowf_h, rowi_h,
    mw, bias,
    out_h, sg_h, mg_out, bg_out,
    field, cot, pgr, mix, kron, sw, wp, colfwd, colinvt, colinv, colfwdt, rowf, rowi,
    modes, big, strip, pre, xkeep,
    qs, qr, zs, zr, ds, dr, ms, mr, gr, us, ur, sg, mg, pack, prz, pdr, pqr, pgz, pk,
    in_sem, out_sem,
    q_ss, q_rs, z_ss, z_rs, d_ss, d_rs, m_ss, m_rs, g_ss, g_rs, u_ss, u_rs,
    p_ss, p_rs,
):
    dp = lax.axis_index("dp")
    sp = lax.axis_index("space")
    z = lax.rem(sp // 2, NZ)
    q = (sp // 16) * 2 + lax.rem(sp, 2)

    def space_of(qq, zz):
        return (qq // 2) * 16 + zz * 2 + lax.rem(qq, 2)

    def quad_peer(r):
        qq = lax.rem(q + r, NQ)
        return qq, {"space": space_of(qq, z)}

    def z_peer(off):
        zz = lax.rem(z + off, NZ)
        return zz, {"space": space_of(q, zz)}

    def dp_peer(r):
        dd = lax.rem(dp + r, DP)
        return dd, {"dp": dd}

    def remote(src, dst, ss, rs, dev):
        return pltpu.make_async_remote_copy(
            src_ref=src, dst_ref=dst, send_sem=ss, recv_sem=rs,
            device_id=dev, device_id_type=pl.DeviceIdType.MESH,
        )

    loads = [
        pltpu.make_async_copy(colfwd_h, colfwd, in_sem.at[0]),
        *[
            pltpu.make_async_copy(
                field_h.at[0, pl.ds(16 * i, 16)], field.at[pl.ds(16 * i, 16)], in_sem.at[1 + i]
            )
            for i in range(4)
        ],
        pltpu.make_async_copy(rowf_h.at[z], rowf, in_sem.at[5]),
        pltpu.make_async_copy(sw_h, sw, in_sem.at[6]),
        pltpu.make_async_copy(rowi_h.at[z], rowi, in_sem.at[7]),
        pltpu.make_async_copy(colinv_h, colinv, in_sem.at[8]),
        pltpu.make_async_copy(cot_h.at[0], cot, in_sem.at[9]),
        pltpu.make_async_copy(colinvt_h, colinvt, in_sem.at[10]),
        pltpu.make_async_copy(colfwdt_h, colfwdt, in_sem.at[11]),
    ]
    for copy in loads:
        copy.start()

    barrier = pltpu.get_barrier_semaphore()
    for r in range(1, NQ):
        pl.semaphore_signal(barrier, 1, device_id=quad_peer(r)[1], device_id_type=pl.DeviceIdType.MESH)
    for r in range(1, NZ):
        pl.semaphore_signal(barrier, 1, device_id=z_peer(r)[1], device_id_type=pl.DeviceIdType.MESH)
    for r in range(1, DP):
        pl.semaphore_signal(barrier, 1, device_id=dp_peer(r)[1], device_id_type=pl.DeviceIdType.MESH)

    low = lax.broadcasted_iota(jnp.int32, (64, 128), 1) < 64
    sign = jnp.where(low, -1.0, 1.0).astype(F32)
    low128 = lax.broadcasted_iota(jnp.int32, (128, 128), 1) < 64
    sign256 = jnp.where(lax.broadcasted_iota(jnp.int32, (256, 128), 1) < 64, -1.0, 1.0).astype(F32)

    loads[0].wait()
    for i in range(4):
        loads[1 + i].wait()
        for j in range(2):
            rows = field[16 * i + 8 * j : 16 * i + 8 * j + 8].reshape(256, W)
            modes[512 * i + 256 * j : 512 * i + 256 * j + 256, :] = lax.dot_general(
                rows, colfwd[...], NN, preferred_element_type=F32
            )
    pl.semaphore_wait(barrier, NQ + NZ + DP - 3)

    def build_kron(transposed):
        spread = (
            lax.broadcasted_iota(jnp.int32, (1024, 64), 0) // 16
            == lax.broadcasted_iota(jnp.int32, (1024, 64), 1)
        ).astype(F32).astype(BF)
        half = lax.dot_general(
            spread, mw[...], NT if transposed else NN, preferred_element_type=F32
        ).astype(BF)
        same = lax.rem(lax.broadcasted_iota(jnp.int32, (256, 1024), 0), 16) == lax.rem(
            lax.broadcasted_iota(jnp.int32, (256, 1024), 1), 16
        )
        for i in range(4):
            full = lax.dot_general(
                half[256 * i : 256 * i + 256], spread, NT, preferred_element_type=F32
            )
            kron[256 * i : 256 * i + 256, :] = jnp.where(same, full, 0.0).astype(BF)

    def pointwise_tile(source, i):
        hb = pl.multiple_of((i // 4) * 16, 16)
        wq = pl.multiple_of(lax.rem(i, 4) * 256, 256)
        rhs = source[:, pl.ds(hb, 16), pl.ds(wq, 256)].reshape(1024, 256)
        res = lax.dot_general(kron[...], rhs, NN, preferred_element_type=F32)
        mix[:, pl.ds(hb, 16), pl.ds(wq, 256)] = res.reshape(64, 16, 256)

    def mixgrad_tile(i):
        hb = pl.multiple_of((i // 4) * 16, 16)
        cb = pl.multiple_of(lax.rem(i, 4) * 16, 16)
        lhs = field[pl.ds(cb, 16), pl.ds(hb, 16), :].reshape(256, W)
        rhs = pgr[:, pl.ds(hb, 16), :].reshape(1024, W)
        res = lax.dot_general(lhs, rhs, NT, preferred_element_type=F32)
        same = lax.rem(lax.broadcasted_iota(jnp.int32, (256, 1024), 0), 16) == lax.rem(
            lax.broadcasted_iota(jnp.int32, (256, 1024), 1), 16
        )
        res = jnp.where(same, res, 0.0).reshape(16, 16, 1024).sum(1)
        mg[pl.ds(cb, 16), :] = mg[pl.ds(cb, 16), :] + res

    def quad_send(ph):
        def turn(h2, total):
            a = modes[pl.ds(2 * h2, 64, stride=SLAB), :]
            b = modes[pl.ds(2 * h2 + 1, 64, stride=SLAB), :]
            big[pl.ds(pl.multiple_of(h2 * 128, 128), 128), :] = jnp.concatenate([a, b], 0).T
            return total + a + b

        total = lax.fori_loop(0, 16, turn, jnp.zeros((64, 128), F32))

        def chunk(i, carry):
            zc = lax.rem(z + far_first(i), NZ)
            for qq in range(NQ):
                for kr in range(4):
                    v = big[pl.ds((zc * NQ + qq) * 4 + kr, 16, stride=128), :]
                    qs[ph, zc, qq, kr * 16 : kr * 16 + 16, :] = v.astype(BF)
            for r in range(1, NQ):
                qq, dev = quad_peer(r)
                remote(
                    qs.at[ph, zc, qq], qr.at[ph, zc, q], q_ss.at[ph, zc, qq], q_rs.at[ph, zc, q], dev
                ).start()
            qr[ph, zc, q] = qs[ph, zc, q]
            return carry

        lax.fori_loop(0, NZ, chunk, 0)
        return total

    def quad_to_z(ph, idle):
        def chunk(i, carry):
            zc = lax.rem(z + far_first(i), NZ)
            for r in range(1, NQ):
                qq, dev = quad_peer(r)
                remote(
                    qs.at[ph, zc, qq], qr.at[ph, zc, qq], q_ss.at[ph, zc, qq], q_rs.at[ph, zc, qq], dev
                ).wait_recv()
            x = qr[ph, zc].reshape(256, 128)
            b = lax.dot_general(rowf[...], x, NN, preferred_element_type=F32)
            straight = jnp.where(low128, b[0:128], b[384:512])
            crossed = jnp.where(low128, b[128:256], b[256:384])
            zs[ph, zc] = (straight + pltpu.roll(crossed, 64, 1)).astype(BF)

            @pl.when(i < 7)
            def _():
                remote(
                    zs.at[ph, zc], zr.at[ph, z], z_ss.at[ph, zc], z_rs.at[ph, z],
                    {"space": space_of(q, zc)},
                ).start()

            idle(i)
            return carry

        lax.fori_loop(0, NZ, chunk, 0)
        total = zs[ph, z].astype(F32)
        for r in range(1, NZ):
            zz, dev = z_peer(r)
            remote(zs.at[ph, zz], zr.at[ph, zz], z_ss.at[ph, zz], z_rs.at[ph, zz], dev).wait_recv()
            total = total + zr[ph, zz].astype(F32)
        return total.astype(BF)

    def dp_out(ph, src, dst, ss, rs, value):
        src[ph] = value.reshape(DP, 16, 128)
        for r in range(1, DP):
            dd, dev = dp_peer(r)
            remote(src.at[ph, dd], dst.at[ph, dp], ss.at[ph, dd], rs.at[ph, dp], dev).start()
        dst[ph, dp] = src[ph, dp]

    def dp_in(ph, src, dst, ss, rs):
        for r in range(1, DP):
            dd, dev = dp_peer(r)
            remote(src.at[ph, dd], dst.at[ph, dd], ss.at[ph, dd], rs.at[ph, dd], dev).wait_recv()
        return dst[ph].reshape(128, 128)

    row_mk = lax.rem(lax.broadcasted_iota(jnp.int32, (128, 128), 0), 16)
    col_mk = lax.rem(lax.broadcasted_iota(jnp.int32, (128, 128), 1), 16)

    def per_mode(x, dims):
        total = jnp.zeros((128, 128), F32)
        for mk in range(16):
            mine = jnp.where(row_mk == mk, x.astype(F32), 0.0).astype(BF)
            total = total + lax.dot_general(mine, wp[mk], dims, preferred_element_type=F32)
        return total.astype(BF)

    def z_send(ph):
        def one(i, carry):
            zz = lax.rem(z + far_first(i), NZ)
            remote(
                mr.at[ph], gr.at[ph, z], g_ss.at[ph, zz], g_rs.at[ph, z], {"space": space_of(q, zz)}
            ).start()
            return carry

        lax.fori_loop(0, 7, one, 0)
        gr[ph, z] = mr[ph]

    def z_to_quad(ph, idle):
        def source(j, carry):
            zc = lax.rem(z + far_first(7 - j), NZ)

            @pl.when(j > 0)
            def _():
                remote(
                    mr.at[ph], gr.at[ph, zc], g_ss.at[ph, zc], g_rs.at[ph, zc],
                    {"space": space_of(q, lax.rem(z + jnp.maximum(far_first(7 - j), 1), NZ))},
                ).wait_recv()

            t = lax.dot_general(
                rowi[...], gr[ph, zc].reshape(128, 128), NN, preferred_element_type=F32
            )
            v = t[0:256] + pltpu.roll(t[256:512], 64, 1) * sign256
            us[ph, zc] = v.astype(BF).reshape(NQ, 64, 128)
            for r in range(1, NQ):
                qq, dev = quad_peer(r)
                remote(
                    us.at[ph, zc, qq], ur.at[ph, zc, q], u_ss.at[ph, zc, qq], u_rs.at[ph, zc, q], dev
                ).start()
            ur[ph, zc, q] = us[ph, zc, q]
            idle(j)
            return carry

        lax.fori_loop(0, NZ, source, 0)

        def take(j, carry):
            zc = lax.rem(z + far_first(7 - j), NZ)
            for r in range(1, NQ):
                qq, dev = quad_peer(r)
                remote(
                    us.at[ph, zc, qq], ur.at[ph, zc, qq], u_ss.at[ph, zc, qq], u_rs.at[ph, zc, qq], dev
                ).wait_recv()
            for qq in range(NQ):
                for k in range(2):
                    v = ur[ph, zc, qq, k * 32 : k * 32 + 32, :].astype(F32)
                    big[pl.ds((zc * NQ + qq) * 2 + k, SLAB, stride=64), :] = v
            return carry

        lax.fori_loop(0, NZ, take, 0)

        def turn(h2, carry):
            t = big[pl.ds(pl.multiple_of(h2 * 128, 128), 128), :].T
            re, im = t[0:64], t[64:128]
            modes[pl.ds(2 * h2, 64, stride=SLAB), :] = jnp.where(low, re, pltpu.roll(im, 64, 1))
            modes[pl.ds(2 * h2 + 1, 64, stride=SLAB), :] = jnp.where(low, pltpu.roll(re, 64, 1), im)
            return carry

        lax.fori_loop(0, 16, turn, 0)

    def nothing(i):
        pass

    quad_send(0)
    build_kron(True)
    loads[5].wait()
    x = quad_to_z(0, functools.partial(pointwise_tile, field))
    dp_out(0, ds, dr, d_ss, d_rs, x)
    loads[6].wait()
    for m in range(8):
        for k in range(2):
            top = sw[m, k].astype(F32)
            bottom = pltpu.roll(top, 64, 1) * sign
            wp[k * 8 + m] = jnp.concatenate([top, bottom], 0).astype(BF)
    mode_rows = dp_in(0, ds, dr, d_ss, d_rs)
    xkeep[...] = mode_rows
    dp_out(0, ms, mr, m_ss, m_rs, per_mode(mode_rows, NN))
    mg[...] = jnp.zeros_like(mg)
    dp_in(0, ms, mr, m_ss, m_rs)
    z_send(0)
    loads[7].wait()
    z_to_quad(0, nothing)

    loads[8].wait()
    loads[9].wait()
    loads[10].wait()
    c1 = math.sqrt(2.0 / math.pi)
    c3 = c1 * 0.044715

    def section(blk, carry):
        r0 = pl.multiple_of(blk * 256, 256)
        pre[...] = lax.dot_general(
            modes[pl.ds(r0, 256), :].astype(BF), colinv[...], NN, preferred_element_type=F32
        )

        def tile(t, inner):
            ch = blk * 8 + t // 2
            hh = pl.multiple_of(lax.rem(t, 2) * 16, 16)
            v = (
                pre[pl.ds(pl.multiple_of(t * 16, 16), 16), :]
                + mix[ch, pl.ds(hh, 16), :]
                + bias[ch]
            )
            v2 = v * v
            th = jnp.tanh(v * (c1 + c3 * v2))
            slope = (0.5 + 0.5 * th) + (v * (0.5 * c1 + 1.5 * c3 * v2)) * (1.0 - th * th)
            pgr[ch, pl.ds(hh, 16), :] = (cot[ch, pl.ds(hh, 16), :].astype(F32) * slope).astype(BF)
            return inner

        lax.fori_loop(0, 16, tile, 0)
        grads = pgr[pl.ds(pl.multiple_of(blk * 8, 8), 8)].reshape(256, W)
        modes[pl.ds(r0, 256), :] = lax.dot_general(
            grads, colinvt[...], NN, preferred_element_type=F32
        )
        return carry

    lax.fori_loop(0, 8, section, 0)

    total = quad_send(1)
    strip[...] = total.T
    build_kron(False)
    g = quad_to_z(1, mixgrad_tile)
    dp_out(1, ds, dr, d_ss, d_rs, g)

    spread = (
        lax.broadcasted_iota(jnp.int32, (1024, 64), 0) // 16
        == lax.broadcasted_iota(jnp.int32, (1024, 64), 1)
    ).astype(F32).astype(BF)
    part = mg[...]
    hi = part.astype(BF)
    rest = part - hi.astype(F32)
    mid = rest.astype(BF)
    lo = (rest - mid.astype(F32)).astype(BF)
    part = (
        lax.dot_general(hi, spread, NN, preferred_element_type=F32)
        + lax.dot_general(mid, spread, NN, preferred_element_type=F32)
        + lax.dot_general(lo, spread, NN, preferred_element_type=F32)
    )
    bias_row = jnp.concatenate([strip[0:1, :] * 32.0, jnp.zeros((63, 64), F32)], 0)
    pack[...] = jnp.concatenate([part, bias_row], 1).reshape(NZ, 8, 128)
    for r in range(1, NZ):
        zz, dev = z_peer(r)
        remote(pack.at[zz], prz.at[z], p_ss.at[0, zz], p_rs.at[0, z], dev).start()
    prz[z] = pack[z]

    grad_rows = dp_in(1, ds, dr, d_ss, d_rs)
    dp_out(1, ms, mr, m_ss, m_rs, per_mode(grad_rows, NT))

    for r in range(1, NZ):
        zz, dev = z_peer(r)
        remote(pack.at[zz], prz.at[zz], p_ss.at[0, zz], p_rs.at[0, zz], dev).wait_recv()
    pk[0] = prz[...].sum(0)
    for r in range(1, DP):
        dd, dev = dp_peer(r)
        remote(pk.at[0], pdr.at[dp], p_ss.at[1, dd], p_rs.at[1, dp], dev).start()
    pdr[dp] = pk[0]

    x_t = xkeep[...].astype(F32).T
    for m in range(8):
        for k in range(2):
            mine = jnp.where(col_mk == k * 8 + m, x_t, 0.0).astype(BF)
            prod = lax.dot_general(mine, grad_rows, NN, preferred_element_type=F32)
            sg[m, k] = prod[0:64] - pltpu.roll(prod[64:128], 64, 1) * sign
    sg_copy = pltpu.make_async_copy(sg, sg_h, out_sem.at[8])
    sg_copy.start()

    dp_in(1, ms, mr, m_ss, m_rs)
    z_send(1)

    for r in range(1, DP):
        dd, dev = dp_peer(r)
        remote(pk.at[0], pdr.at[dd], p_ss.at[1, dd], p_rs.at[1, dd], dev).wait_recv()
    pk[1] = pdr[...].sum(0)
    for r in range(1, NQ):
        qq, dev = quad_peer(r)
        remote(pk.at[1], pqr.at[q], p_ss.at[2, qq], p_rs.at[2, q], dev).start()
    pqr[q] = pk[1]

    z_to_quad(1, functools.partial(pointwise_tile, pgr))

    for r in range(1, NQ):
        qq, dev = quad_peer(r)
        remote(pk.at[1], pqr.at[qq], p_ss.at[2, qq], p_rs.at[2, qq], dev).wait_recv()
    pk[2] = pqr[...].sum(0)
    for r in range(1, NZ):
        zz, dev = z_peer(r)
        remote(pk.at[2], pgz.at[z], p_ss.at[3, zz], p_rs.at[3, z], dev).start()
    pgz[z] = pk[2]

    loads[11].wait()
    for blk in range(8):
        rows = lax.dot_general(
            modes[256 * blk : 256 * blk + 256, :].astype(BF), colfwdt[...], NN,
            preferred_element_type=F32,
        )
        chs = slice(8 * blk, 8 * blk + 8)
        cot[chs] = (rows.reshape(8, SLAB, W) + mix[chs]).astype(BF)
        pltpu.make_async_copy(cot.at[chs], out_h.at[0, chs], out_sem.at[blk]).start()

    for r in range(1, NZ):
        zz, dev = z_peer(r)
        remote(pk.at[2], pgz.at[zz], p_ss.at[3, zz], p_rs.at[3, zz], dev).wait_recv()
    norm = 1.0 / math.sqrt(DP * H * W)
    whole = pgz[...].reshape(64, 128) * norm
    mg_out[...] = whole[:, 0:64]
    bg_out[...] = whole[0:1, 64:128]

    for ph in range(2):

        def drain(i, carry):
            for r in range(1, NQ):
                qq, dev = quad_peer(r)
                remote(
                    qs.at[ph, i, qq], qr.at[ph, i, q], q_ss.at[ph, i, qq], q_rs.at[ph, i, q], dev
                ).wait_send()
                remote(
                    us.at[ph, i, qq], ur.at[ph, i, q], u_ss.at[ph, i, qq], u_rs.at[ph, i, q], dev
                ).wait_send()
            return carry

        lax.fori_loop(0, NZ, drain, 0)
        for r in range(1, NZ):
            zz, dev = z_peer(r)
            remote(zs.at[ph, zz], zr.at[ph, z], z_ss.at[ph, zz], z_rs.at[ph, z], dev).wait_send()
            remote(mr.at[ph], gr.at[ph, z], g_ss.at[ph, zz], g_rs.at[ph, z], dev).wait_send()
            dd, dev = dp_peer(r)
            remote(ds.at[ph, dd], dr.at[ph, dp], d_ss.at[ph, dd], d_rs.at[ph, dp], dev).wait_send()
            remote(ms.at[ph, dd], mr.at[ph, dp], m_ss.at[ph, dd], m_rs.at[ph, dp], dev).wait_send()
    for r in range(1, NZ):
        zz, dev = z_peer(r)
        remote(pack.at[zz], prz.at[z], p_ss.at[0, zz], p_rs.at[0, z], dev).wait_send()
        remote(pk.at[2], pgz.at[z], p_ss.at[3, zz], p_rs.at[3, z], dev).wait_send()
        dd, dev = dp_peer(r)
        remote(pk.at[0], pdr.at[dp], p_ss.at[1, dd], p_rs.at[1, dp], dev).wait_send()
    for r in range(1, NQ):
        qq, dev = quad_peer(r)
        remote(pk.at[1], pqr.at[q], p_ss.at[2, qq], p_rs.at[2, q], dev).wait_send()
    for blk in range(8):
        chs = slice(8 * blk, 8 * blk + 8)
        pltpu.make_async_copy(cot.at[chs], out_h.at[0, chs], out_sem.at[blk]).wait()
    sg_copy.wait()


def per_device(field, cotangent, spectral_weight, mixing_weight, bias):
    tables = [jnp.asarray(t) for t in build_tables()]
    hbm = pl.BlockSpec(memory_space=pl.ANY)
    vmem = pl.BlockSpec(memory_space=pltpu.VMEM)
    smem = pl.BlockSpec(memory_space=pltpu.SMEM)
    dma = pltpu.SemaphoreType.DMA
    out = pl.pallas_call(
        kernel,
        out_shape=(
            jax.ShapeDtypeStruct((1, C, SLAB, W), BF),
            jax.ShapeDtypeStruct((8, 2, C, 2 * C), F32),
            jax.ShapeDtypeStruct((C, C), F32),
            jax.ShapeDtypeStruct((1, C), F32),
        ),
        in_specs=[hbm] * 9 + [vmem, smem],
        out_specs=(hbm, hbm, vmem, vmem),
        scratch_shapes=[
            pltpu.VMEM((C, SLAB, W), BF),
            pltpu.VMEM((C, SLAB, W), BF),
            pltpu.VMEM((C, SLAB, W), BF),
            pltpu.VMEM((C, SLAB, W), F32),
            pltpu.VMEM((1024, 1024), BF),
            pltpu.VMEM((8, 2, C, 2 * C), BF),
            pltpu.VMEM((16, 128, 128), BF),
            pltpu.VMEM((W, 128), BF),
            pltpu.VMEM((W, 128), BF),
            pltpu.VMEM((128, W), BF),
            pltpu.VMEM((128, W), BF),
            pltpu.VMEM((512, 256), BF),
            pltpu.VMEM((512, 128), BF),
            pltpu.VMEM((C * SLAB, 128), F32),
            pltpu.VMEM((C * SLAB, 128), F32),
            pltpu.VMEM((128, C), F32),
            pltpu.VMEM((256, W), F32),
            pltpu.VMEM((128, 128), BF),
            pltpu.VMEM((2, NZ, NQ, 64, 128), BF),
            pltpu.VMEM((2, NZ, NQ, 64, 128), BF),
            pltpu.VMEM((2, NZ, 128, 128), BF),
            pltpu.VMEM((2, NZ, 128, 128), BF),
            pltpu.VMEM((2, DP, 16, 128), BF),
            pltpu.VMEM((2, DP, 16, 128), BF),
            pltpu.VMEM((2, DP, 16, 128), BF),
            pltpu.VMEM((2, DP, 16, 128), BF),
            pltpu.VMEM((2, NZ, DP, 16, 128), BF),
            pltpu.VMEM((2, NZ, NQ, 64, 128), BF),
            pltpu.VMEM((2, NZ, NQ, 64, 128), BF),
            pltpu.VMEM((8, 2, C, 2 * C), F32),
            pltpu.VMEM((C, 1024), F32),
            pltpu.VMEM((NZ, 8, 128), F32),
            pltpu.VMEM((NZ, 8, 128), F32),
            pltpu.VMEM((DP, 8, 128), F32),
            pltpu.VMEM((NQ, 8, 128), F32),
            pltpu.VMEM((NZ, 8, 128), F32),
            pltpu.VMEM((3, 8, 128), F32),
            dma((12,)),
            dma((9,)),
            dma((2, NZ, NQ)), dma((2, NZ, NQ)),
            dma((2, NZ)), dma((2, NZ)),
            dma((2, DP)), dma((2, DP)),
            dma((2, DP)), dma((2, DP)),
            dma((2, NZ)), dma((2, NZ)),
            dma((2, NZ, NQ)), dma((2, NZ, NQ)),
            dma((4, 8)), dma((4, 8)),
        ],
        compiler_params=pltpu.CompilerParams(
            collective_id=0, has_side_effects=True, vmem_limit_bytes=58 * 1024 * 1024
        ),
        cost_estimate=pl.CostEstimate(
            flops=20_000_000_000, bytes_accessed=16_000_000, transcendentals=2_000_000
        ),
    )(field, cotangent, spectral_weight, *tables, mixing_weight, bias)
    field_grad, spectral_grad, mixing_grad, bias_grad = out
    return field_grad, spectral_grad, mixing_grad, bias_grad.reshape(C)


def solution(mesh):
    return jax.shard_map(
        per_device,
        mesh=mesh,
        in_specs=(
            P("dp", None, "space", None),
            P("dp", None, "space", None),
            P("dp", "space", None, None),
            P(),
            P(),
        ),
        out_specs=(P("dp", None, "space", None), P("dp", "space", None, None), P(), P()),
        check_vma=False,
    )
```

```python
import functools
import math

import jax
import jax.numpy as jnp
import ml_dtypes
import numpy as np
from jax import lax
from jax.experimental import pallas as pl
from jax.experimental.pallas import tpu as pltpu
from jax.sharding import PartitionSpec as P

C = 64
H = 1024
W = 1024
K1 = 64
K2 = 64
DP = 8
NZ = 8
NQ = 4
SLAB = 32
BF = jnp.bfloat16
F32 = jnp.float32
NN = (((1,), (0,)), ((), ()))
NT = (((1,), (1,)), ((), ()))


def build_tables():
    f32 = np.float32
    wpos = np.arange(W)[:, None]
    kpos = np.arange(K2)[None, :]
    angle = (wpos * kpos % W).astype(f32) * f32(2.0 * math.pi / W)
    scale = f32(1.0 / math.sqrt(W))
    cosine = np.cos(angle) * scale
    sine = np.sin(angle) * scale
    factor = np.where(kpos == 0, 1.0, 2.0).astype(f32)
    fwd = np.stack([cosine, -sine], 0).astype(ml_dtypes.bfloat16)
    inv = np.stack([factor * cosine, -factor * sine], 0).astype(ml_dtypes.bfloat16)
    z, xl, core, kk = np.meshgrid(
        np.arange(NZ), np.arange(2), np.arange(2), np.arange(2), indexing="ij"
    )
    order = (2 * (xl * 16 + z * 2 + core) + kk).reshape(-1)
    colfwd = fwd[:, :, order].transpose(1, 2, 0).reshape(W, 2 * K2)
    colinv_t = inv[:, :, order].transpose(1, 2, 0).reshape(W, 2 * K2)
    colinv = inv[:, :, order].transpose(0, 2, 1).reshape(2 * K2, W)
    colfwd_t = fwd[:, :, order].transpose(0, 2, 1).reshape(2 * K2, W)

    mpos = np.arange(K1)[:, None]
    freq = mpos + np.where(mpos >= K1 // 2, H - K1, 0)
    hpos = np.arange(H)[None, :]
    phase = (freq * hpos % H).astype(f32) * f32(2.0 * math.pi / H)
    rc = (np.cos(phase) / f32(math.sqrt(H))).astype(ml_dtypes.bfloat16)
    rs = (np.sin(phase) / f32(math.sqrt(H))).astype(ml_dtypes.bfloat16)
    fwd_rows = []
    inv_rows = []
    for zi in range(NZ):
        slabs = np.array([x * 16 + zi * 2 + c for x in range(2) for c in range(2)])
        rows = slabs[:, None, None] * SLAB + np.arange(16)[None, :, None] * 2 + np.arange(2)
        ct = rc[:, rows].reshape(DP, 8, NQ, 16, 2)
        st = rs[:, rows].reshape(DP, 8, NQ, 16, 2)
        big = np.zeros((2, 2, DP, 2, 8, NQ, 2, 2, 16), ml_dtypes.bfloat16)
        for hl in range(2):
            for k in range(2):
                big[hl, 0, :, k, :, :, k, 0] = ct[..., hl]
                big[hl, 0, :, k, :, :, k, 1] = st[..., hl]
                big[hl, 1, :, k, :, :, k, 0] = -st[..., hl]
                big[hl, 1, :, k, :, :, k, 1] = ct[..., hl]
        fwd_rows.append(big.reshape(512, 256))
        rows = slabs[:, None] * SLAB + np.arange(SLAB)[None, :]
        tab = np.zeros((2, NQ, 2, SLAB, DP, 2, 8), ml_dtypes.bfloat16)
        for i, t in enumerate((rc, rs)):
            v = t[:, rows].reshape(DP, 8, NQ, SLAB).transpose(2, 3, 0, 1)
            for k in range(2):
                tab[i, :, k, :, :, k, :] = v
        inv_rows.append(tab.reshape(512, 128))
    i = np.arange(256)
    sources = (
        32 * (i % 8) + i // 8,
        8 * (i % 32) + i // 32,
        16 * (i % 16) + i // 16,
    )
    perms = np.stack([np.eye(256)[s] for s in sources]).astype(ml_dtypes.bfloat16)
    return colfwd, colinv_t, colinv, colfwd_t, np.stack(fwd_rows), np.stack(inv_rows), perms


def far_first(i):
    step = (i + 1) // 2
    return lax.rem(4 + step * (2 * lax.rem(i, 2) - 1) + 8, 8)


def kernel(
    field_h, cot_h, sw_h, colfwd_h, colinvt_h, colinv_h, rowf_h, rowi_h, perm_h,
    mw, bias,
    pm_h, l_h, sg_h, mg_out, bg_out,
    field, cot, pgr, mix, kron, sw, wp, colfwd, colinvt, colinv, rowf, rowi,
    perm, slab, big, back, lrows, pre0, pre1, xkeep, strip,
    qs, qr, zs, zr, ds, dr, ms, mr, gr, us, ur, sg, mg, pack, prz, pdr, pqr, pgz, pk,
    in_sem, out_sem,
    q_ss, q_rs, z_ss, z_rs, d_ss, d_rs, m_ss, m_rs, g_ss, g_rs, u_ss, u_rs,
    p_ss, p_rs,
):
    dp = lax.axis_index("dp")
    sp = lax.axis_index("space")
    z = lax.rem(sp // 2, NZ)
    q = (sp // 16) * 2 + lax.rem(sp, 2)

    def space_of(qq, zz):
        return (qq // 2) * 16 + zz * 2 + lax.rem(qq, 2)

    def quad_peer(r):
        qq = lax.rem(q + r, NQ)
        return qq, {"space": space_of(qq, z)}

    def z_peer(off):
        zz = lax.rem(z + off, NZ)
        return zz, {"space": space_of(q, zz)}

    def dp_peer(r):
        dd = lax.rem(dp + r, DP)
        return dd, {"dp": dd}

    def remote(src, dst, ss, rs, dev):
        return pltpu.make_async_remote_copy(
            src_ref=src, dst_ref=dst, send_sem=ss, recv_sem=rs,
            device_id=dev, device_id_type=pl.DeviceIdType.MESH,
        )

    loads = [
        pltpu.make_async_copy(colfwd_h, colfwd, in_sem.at[0]),
        *[
            pltpu.make_async_copy(
                field_h.at[0, pl.ds(8 * i, 8)], field.at[pl.ds(8 * i, 8)], in_sem.at[1 + i]
            )
            for i in range(8)
        ],
        pltpu.make_async_copy(perm_h, perm, in_sem.at[15]),
        pltpu.make_async_copy(rowf_h.at[z], rowf, in_sem.at[9]),
        pltpu.make_async_copy(sw_h, sw, in_sem.at[10]),
        pltpu.make_async_copy(rowi_h.at[z], rowi, in_sem.at[11]),
        pltpu.make_async_copy(colinv_h, colinv, in_sem.at[12]),
        pltpu.make_async_copy(colinvt_h, colinvt, in_sem.at[13]),
        pltpu.make_async_copy(cot_h.at[0], cot, in_sem.at[14]),
    ]
    for copy in loads[:11]:
        copy.start()

    barrier = pltpu.get_barrier_semaphore()
    for r in range(1, NQ):
        pl.semaphore_signal(barrier, 1, device_id=quad_peer(r)[1], device_id_type=pl.DeviceIdType.MESH)
    for r in range(1, NZ):
        pl.semaphore_signal(barrier, 1, device_id=z_peer(r)[1], device_id_type=pl.DeviceIdType.MESH)
    for r in range(1, DP):
        pl.semaphore_signal(barrier, 1, device_id=dp_peer(r)[1], device_id_type=pl.DeviceIdType.MESH)

    low = lax.broadcasted_iota(jnp.int32, (64, 128), 1) < 64
    sign = jnp.where(low, -1.0, 1.0).astype(F32)
    low128 = lax.broadcasted_iota(jnp.int32, (128, 128), 1) < 64
    sign256 = jnp.where(lax.broadcasted_iota(jnp.int32, (256, 128), 1) < 64, -1.0, 1.0).astype(F32)

    def to_slab(blk, rows):
        res = lax.dot_general(perm[0], rows.astype(BF), NN, preferred_element_type=F32)
        slab[:, pl.ds(blk * 8 if isinstance(blk, int) else pl.multiple_of(blk * 8, 8), 8), :] = (
            res.reshape(SLAB, 8, 128)
        )

    def from_slab(blk):
        start = blk * 8 if isinstance(blk, int) else pl.multiple_of(blk * 8, 8)
        rows = slab[:, pl.ds(start, 8), :].reshape(256, 128).astype(BF)
        return lax.dot_general(perm[1], rows, NN, preferred_element_type=F32).astype(BF)

    loads[0].wait()
    loads[9].wait()
    for i in range(8):
        loads[1 + i].wait()
        rows = field[8 * i : 8 * i + 8].reshape(256, W)
        to_slab(i, lax.dot_general(rows, colfwd[...], NN, preferred_element_type=F32))
    for copy in loads[11:]:
        copy.start()
    pl.semaphore_wait(barrier, NQ + NZ + DP - 3)

    def build_kron(n, transposed):
        spread = (
            lax.broadcasted_iota(jnp.int32, (1024, 64), 0) // 16
            == lax.broadcasted_iota(jnp.int32, (1024, 64), 1)
        ).astype(F32).astype(BF)
        half = lax.dot_general(
            spread, mw[...], NT if transposed else NN, preferred_element_type=F32
        ).astype(BF)
        same = lax.rem(lax.broadcasted_iota(jnp.int32, (256, 1024), 0), 16) == lax.rem(
            lax.broadcasted_iota(jnp.int32, (256, 1024), 1), 16
        )
        for i in range(4):
            full = lax.dot_general(
                half[256 * i : 256 * i + 256], spread, NT, preferred_element_type=F32
            )
            kron[n, 256 * i : 256 * i + 256, :] = jnp.where(same, full, 0.0).astype(BF)

    def pointwise_tile(n, source, target, i):
        hb = pl.multiple_of((i // 4) * 16, 16)
        wq = pl.multiple_of(lax.rem(i, 4) * 256, 256)
        rhs = source[:, pl.ds(hb, 16), pl.ds(wq, 256)].reshape(1024, 256)
        res = lax.dot_general(kron[n], rhs, NN, preferred_element_type=F32)
        target[:, pl.ds(hb, 16), pl.ds(wq, 256)] = res.reshape(64, 16, 256).astype(target.dtype)

    def some(tile, first, last):
        def one(i, carry):
            tile(i)
            return carry

        lax.fori_loop(first, last, one, 0)

    def mixgrad_tile(i):
        hb = pl.multiple_of((i // 4) * 16, 16)
        cb = pl.multiple_of(lax.rem(i, 4) * 16, 16)
        lhs = field[pl.ds(cb, 16), pl.ds(hb, 16), :].reshape(256, W)
        rhs = pgr[:, pl.ds(hb, 16), :].reshape(1024, W)
        res = lax.dot_general(lhs, rhs, NT, preferred_element_type=F32)
        same = lax.rem(lax.broadcasted_iota(jnp.int32, (256, 1024), 0), 16) == lax.rem(
            lax.broadcasted_iota(jnp.int32, (256, 1024), 1), 16
        )
        res = jnp.where(same, res, 0.0).reshape(16, 16, 1024).sum(1)
        mg[pl.ds(cb, 16), :] = mg[pl.ds(cb, 16), :] + res

    def quad_send(ph):
        for h2 in range(16):
            big[h2] = slab[2 * h2 : 2 * h2 + 2].reshape(128, 128).T.astype(BF)
        for zc in range(NZ):
            rows = big[:, zc * 16 : zc * 16 + 16, :].reshape(256, 128)
            res = lax.dot_general(perm[2], rows, NN, preferred_element_type=F32)
            qs[ph, zc] = res.astype(BF).reshape(NQ, 64, 128)

        def chunk(i, carry):
            zc = lax.rem(z + far_first(i), NZ)
            for r in range(1, NQ):
                qq, dev = quad_peer(r)
                remote(
                    qs.at[ph, zc, qq], qr.at[ph, zc, q], q_ss.at[ph, zc, qq], q_rs.at[ph, zc, q], dev
                ).start()
            qr[ph, zc, q] = qs[ph, zc, q]
            return carry

        lax.fori_loop(0, NZ, chunk, 0)

    def quad_to_z(ph):
        def chunk(i, carry):
            zc = lax.rem(z + far_first(i), NZ)
            for r in range(1, NQ):
                qq, dev = quad_peer(r)
                remote(
                    qs.at[ph, zc, qq], qr.at[ph, zc, qq], q_ss.at[ph, zc, qq], q_rs.at[ph, zc, qq], dev
                ).wait_recv()
            x = qr[ph, zc].reshape(256, 128)
            b = lax.dot_general(rowf[...], x, NN, preferred_element_type=F32)
            straight = jnp.where(low128, b[0:128], b[384:512])
            crossed = jnp.where(low128, b[128:256], b[256:384])
            zs[ph, zc] = (straight + pltpu.roll(crossed, 64, 1)).astype(BF)

            @pl.when(i < 7)
            def _():
                remote(
                    zs.at[ph, zc], zr.at[ph, z], z_ss.at[ph, zc], z_rs.at[ph, z],
                    {"space": space_of(q, zc)},
                ).start()

            return carry

        lax.fori_loop(0, NZ, chunk, 0)

    def z_sum(ph):
        total = zs[ph, z].astype(F32)
        for r in range(1, NZ):
            zz, dev = z_peer(r)
            remote(zs.at[ph, zz], zr.at[ph, zz], z_ss.at[ph, zz], z_rs.at[ph, zz], dev).wait_recv()
            total = total + zr[ph, zz].astype(F32)
        return total.astype(BF)

    def dp_out(ph, src, dst, ss, rs, value):
        src[ph] = value.reshape(DP, 16, 128)
        for r in range(1, DP):
            dd, dev = dp_peer(r)
            remote(src.at[ph, dd], dst.at[ph, dp], ss.at[ph, dd], rs.at[ph, dp], dev).start()
        dst[ph, dp] = src[ph, dp]

    def dp_in(ph, src, dst, ss, rs):
        for r in range(1, DP):
            dd, dev = dp_peer(r)
            remote(src.at[ph, dd], dst.at[ph, dd], ss.at[ph, dd], rs.at[ph, dd], dev).wait_recv()
        return dst[ph].reshape(128, 128)

    row_mk = lax.rem(lax.broadcasted_iota(jnp.int32, (128, 128), 0), 16)
    col_mk = lax.rem(lax.broadcasted_iota(jnp.int32, (128, 128), 1), 16)

    def per_mode(x, dims):
        total = jnp.zeros((128, 128), F32)
        for mk in range(16):
            mine = jnp.where(row_mk == mk, x.astype(F32), 0.0).astype(BF)
            total = total + lax.dot_general(mine, wp[mk], dims, preferred_element_type=F32)
        return total.astype(BF)

    def z_send(ph):
        def one(i, carry):
            zz = lax.rem(z + far_first(i), NZ)
            remote(
                mr.at[ph], gr.at[ph, z], g_ss.at[ph, zz], g_rs.at[ph, z], {"space": space_of(q, zz)}
            ).start()
            return carry

        lax.fori_loop(0, 7, one, 0)
        gr[ph, z] = mr[ph]

    def z_to_quad(ph, early, between):
        def source(j, carry):
            j = jnp.int32(j)
            zc = lax.rem(z + far_first(7 - j), NZ)

            @pl.when(j > 0)
            def _():
                remote(
                    mr.at[ph], gr.at[ph, zc], g_ss.at[ph, zc], g_rs.at[ph, zc],
                    {"space": space_of(q, lax.rem(z + jnp.maximum(far_first(7 - j), 1), NZ))},
                ).wait_recv()

            t = lax.dot_general(
                rowi[...], gr[ph, zc].reshape(128, 128), NN, preferred_element_type=F32
            )
            v = t[0:256] + pltpu.roll(t[256:512], 64, 1) * sign256
            us[ph, zc] = v.astype(BF).reshape(NQ, 64, 128)
            for r in range(1, NQ):
                qq, dev = quad_peer(r)
                remote(
                    us.at[ph, zc, qq], ur.at[ph, zc, q], u_ss.at[ph, zc, qq], u_rs.at[ph, zc, q], dev
                ).start()
            ur[ph, zc, q] = us[ph, zc, q]
            return carry

        source(0, 0)
        early()
        lax.fori_loop(1, NZ, source, 0)
        between()

        def take(j, carry):
            zc = lax.rem(z + far_first(7 - j), NZ)
            for r in range(1, NQ):
                qq, dev = quad_peer(r)
                remote(
                    us.at[ph, zc, qq], ur.at[ph, zc, qq], u_ss.at[ph, zc, qq], u_rs.at[ph, zc, qq], dev
                ).wait_recv()
            res = lax.dot_general(
                perm[0], ur[ph, zc].reshape(256, 128), NN, preferred_element_type=F32
            )
            back[:, pl.ds(pl.multiple_of(zc * 8, 8), 8), :] = res.reshape(SLAB, 8, 128)
            return carry

        lax.fori_loop(0, NZ, take, 0)
        for h2 in range(16):
            t = back[2 * h2 : 2 * h2 + 2].reshape(128, 128).T
            re, im = t[0:64], t[64:128]
            slab[2 * h2] = jnp.where(low, re, pltpu.roll(im, 64, 1))
            slab[2 * h2 + 1] = jnp.where(low, pltpu.roll(re, 64, 1), im)

    field_mix = functools.partial(pointwise_tile, 0, field, mix)
    grad_mix = functools.partial(pointwise_tile, 1, pgr, cot)

    quad_send(0)
    build_kron(0, True)
    loads[10].wait()
    quad_to_z(0)
    some(field_mix, 0, 2)
    x = z_sum(0)
    dp_out(0, ds, dr, d_ss, d_rs, x)
    loads[11].wait()
    for m in range(8):
        for k in range(2):
            top = sw[m, k].astype(F32)
            bottom = pltpu.roll(top, 64, 1) * sign
            wp[k * 8 + m] = jnp.concatenate([top, bottom], 0).astype(BF)
    some(field_mix, 2, 5)
    mode_rows = dp_in(0, ds, dr, d_ss, d_rs)
    xkeep[...] = mode_rows
    dp_out(0, ms, mr, m_ss, m_rs, per_mode(mode_rows, NN))
    some(field_mix, 5, 8)
    mg[...] = jnp.zeros_like(mg)
    dp_in(0, ms, mr, m_ss, m_rs)
    z_send(0)
    loads[12].wait()

    def late_loads():
        for copy in loads[13:]:
            copy.wait()

    z_to_quad(0, functools.partial(build_kron, 1, False), late_loads)

    c1 = math.sqrt(2.0 / math.pi)
    c3 = c1 * 0.044715

    def pre_part(blk, pre):
        pre[...] = lax.dot_general(from_slab(blk), colinv[...], NN, preferred_element_type=F32)

    def slopes(blk, pre):
        for t in range(16):
            ch = blk * 8 + t // 2
            hh = slice(16 * (t % 2), 16 * (t % 2) + 16)
            v = pre[16 * t : 16 * t + 16, :] + mix[ch, hh, :] + bias[ch]
            v2 = v * v
            a = 0.5 + 0.5 * jnp.tanh(v * (c1 + c3 * v2))
            slope = a + a * (1.0 - a) * (v * (2.0 * c1 + 6.0 * c3 * v2))
            pgr[ch, hh, :] = (cot[ch, hh, :].astype(F32) * slope).astype(BF)

    def grad_part(blk):
        grads = pgr[pl.ds(pl.multiple_of(blk * 8, 8), 8)].reshape(256, W)
        rows = lax.dot_general(grads, colinvt[...], NN, preferred_element_type=F32)
        to_slab(blk, rows)
        strip[pl.ds(pl.multiple_of(blk * 8, 8), 8), :] = rows.reshape(8, SLAB, 128).sum(1)

    pre_part(0, pre0)

    def section(i, carry):
        blk = 2 * i
        pre_part(blk + 1, pre1)
        slopes(blk, pre0)
        grad_part(blk)
        pre_part(jnp.minimum(blk + 2, 6), pre0)
        slopes(blk + 1, pre1)
        grad_part(blk + 1)
        return carry

    lax.fori_loop(0, 4, section, 0)

    quad_send(1)
    quad_to_z(1)
    some(mixgrad_tile, 0, 3)
    g = z_sum(1)
    dp_out(1, ds, dr, d_ss, d_rs, g)
    some(mixgrad_tile, 3, 8)
    grad_rows = dp_in(1, ds, dr, d_ss, d_rs)
    dp_out(1, ms, mr, m_ss, m_rs, per_mode(grad_rows, NT))

    spread = (
        lax.broadcasted_iota(jnp.int32, (1024, 64), 0) // 16
        == lax.broadcasted_iota(jnp.int32, (1024, 64), 1)
    ).astype(F32).astype(BF)
    part = mg[...]
    hi = part.astype(BF)
    rest = part - hi.astype(F32)
    mid = rest.astype(BF)
    lo = (rest - mid.astype(F32)).astype(BF)
    part = (
        lax.dot_general(hi, spread, NN, preferred_element_type=F32)
        + lax.dot_general(mid, spread, NN, preferred_element_type=F32)
        + lax.dot_general(lo, spread, NN, preferred_element_type=F32)
    )
    bias_row = strip[...].T[0:1, :] * 32.0
    pack[...] = jnp.concatenate(
        [part, jnp.concatenate([bias_row, jnp.zeros((63, 64), F32)], 0)], 1
    ).reshape(NZ, 8, 128)
    for r in range(1, NZ):
        zz, dev = z_peer(r)
        remote(pack.at[zz], prz.at[z], p_ss.at[0, zz], p_rs.at[0, z], dev).start()
    prz[z] = pack[z]

    some(grad_mix, 0, 4)

    for r in range(1, NZ):
        zz, dev = z_peer(r)
        remote(pack.at[zz], prz.at[zz], p_ss.at[0, zz], p_rs.at[0, zz], dev).wait_recv()
    pk[0] = prz[...].sum(0)
    for r in range(1, DP):
        dd, dev = dp_peer(r)
        remote(pk.at[0], pdr.at[dp], p_ss.at[1, dd], p_rs.at[1, dp], dev).start()
    pdr[dp] = pk[0]

    dp_in(1, ms, mr, m_ss, m_rs)
    z_send(1)

    pm_copy = pltpu.make_async_copy(cot, pm_h, out_sem.at[1])

    sg_copy = pltpu.make_async_copy(sg, sg_h, out_sem.at[0])

    def early():
        some(grad_mix, 4, 7)

        for r in range(1, DP):
            dd, dev = dp_peer(r)
            remote(pk.at[0], pdr.at[dd], p_ss.at[1, dd], p_rs.at[1, dd], dev).wait_recv()
        pk[1] = pdr[...].sum(0)
        for r in range(1, NQ):
            qq, dev = quad_peer(r)
            remote(pk.at[1], pqr.at[q], p_ss.at[2, qq], p_rs.at[2, q], dev).start()
        pqr[q] = pk[1]

    def totals():
        x_t = xkeep[...].astype(F32).T
        for m in range(8):
            for k in range(2):
                mine = jnp.where(col_mk == k * 8 + m, x_t, 0.0).astype(BF)
                prod = lax.dot_general(mine, grad_rows, NN, preferred_element_type=F32)
                sg[m, k] = prod[0:64] - pltpu.roll(prod[64:128], 64, 1) * sign
        sg_copy.start()
        some(grad_mix, 7, 8)
        pm_copy.start()
        for r in range(1, NQ):
            qq, dev = quad_peer(r)
            remote(pk.at[1], pqr.at[qq], p_ss.at[2, qq], p_rs.at[2, qq], dev).wait_recv()
        pk[2] = pqr[...].sum(0)
        for r in range(1, NZ):
            zz, dev = z_peer(r)
            remote(pk.at[2], pgz.at[z], p_ss.at[3, zz], p_rs.at[3, z], dev).start()
        pgz[z] = pk[2]

    z_to_quad(1, early, totals)

    for blk in range(8):
        lrows[256 * blk : 256 * blk + 256, :] = from_slab(blk)
    l_copy = pltpu.make_async_copy(lrows, l_h, out_sem.at[2])
    l_copy.start()

    for r in range(1, NZ):
        zz, dev = z_peer(r)
        remote(pk.at[2], pgz.at[zz], p_ss.at[3, zz], p_rs.at[3, zz], dev).wait_recv()
    norm = 1.0 / math.sqrt(DP * H * W)
    whole = pgz[...].reshape(64, 128) * norm
    mg_out[...] = whole[:, 0:64]
    bg_out[...] = whole[0:1, 64:128]

    for ph in range(2):

        def drain(i, carry):
            for r in range(1, NQ):
                qq, dev = quad_peer(r)
                remote(
                    qs.at[ph, i, qq], qr.at[ph, i, q], q_ss.at[ph, i, qq], q_rs.at[ph, i, q], dev
                ).wait_send()
                remote(
                    us.at[ph, i, qq], ur.at[ph, i, q], u_ss.at[ph, i, qq], u_rs.at[ph, i, q], dev
                ).wait_send()
            return carry

        lax.fori_loop(0, NZ, drain, 0)
        for r in range(1, NZ):
            zz, dev = z_peer(r)
            remote(zs.at[ph, zz], zr.at[ph, z], z_ss.at[ph, zz], z_rs.at[ph, z], dev).wait_send()
            remote(mr.at[ph], gr.at[ph, z], g_ss.at[ph, zz], g_rs.at[ph, z], dev).wait_send()
            dd, dev = dp_peer(r)
            remote(ds.at[ph, dd], dr.at[ph, dp], d_ss.at[ph, dd], d_rs.at[ph, dp], dev).wait_send()
            remote(ms.at[ph, dd], mr.at[ph, dp], m_ss.at[ph, dd], m_rs.at[ph, dp], dev).wait_send()
    for r in range(1, NZ):
        zz, dev = z_peer(r)
        remote(pack.at[zz], prz.at[z], p_ss.at[0, zz], p_rs.at[0, z], dev).wait_send()
        remote(pk.at[2], pgz.at[z], p_ss.at[3, zz], p_rs.at[3, z], dev).wait_send()
        dd, dev = dp_peer(r)
        remote(pk.at[0], pdr.at[dp], p_ss.at[1, dd], p_rs.at[1, dp], dev).wait_send()
    for r in range(1, NQ):
        qq, dev = quad_peer(r)
        remote(pk.at[1], pqr.at[q], p_ss.at[2, qq], p_rs.at[2, q], dev).wait_send()
    sg_copy.wait()
    pm_copy.wait()
    l_copy.wait()


def finish(pm_h, l_h, colfwdt_h, sg_h, mg_in, bg_in, out_h, sg_out, mg_out, bg_out,
           pm, lrows, colfwdt, sg, in_sem, out_sem):
    loads = [
        pltpu.make_async_copy(l_h, lrows, in_sem.at[8]),
        pltpu.make_async_copy(colfwdt_h, colfwdt, in_sem.at[9]),
        *[
            pltpu.make_async_copy(pm_h.at[pl.ds(8 * i, 8)], pm.at[pl.ds(8 * i, 8)], in_sem.at[i])
            for i in range(8)
        ],
        pltpu.make_async_copy(sg_h, sg, in_sem.at[10]),
    ]
    for copy in loads:
        copy.start()
    mg_out[...] = mg_in[...]
    bg_out[...] = bg_in[...]
    loads[0].wait()
    loads[1].wait()
    stores = []
    for i in range(8):
        rows = lax.dot_general(
            lrows[256 * i : 256 * i + 256, :], colfwdt[...], NN, preferred_element_type=F32
        )
        loads[2 + i].wait()
        chs = slice(8 * i, 8 * i + 8)
        pm[chs] = (rows.reshape(8, SLAB, W) + pm[chs].astype(F32)).astype(BF)
        stores.append(pltpu.make_async_copy(pm.at[chs], out_h.at[0, chs], out_sem.at[i]))
        stores[-1].start()
    loads[10].wait()
    stores.append(pltpu.make_async_copy(sg, sg_out, out_sem.at[8]))
    stores[-1].start()
    for copy in stores:
        copy.wait()


def per_device(field, cotangent, spectral_weight, mixing_weight, bias):
    colfwd, colinv_t, colinv, colfwd_t, row_fwd, row_inv, perms = [
        jnp.asarray(t) for t in build_tables()
    ]
    hbm = pl.BlockSpec(memory_space=pl.ANY)
    vmem = pl.BlockSpec(memory_space=pltpu.VMEM)
    smem = pl.BlockSpec(memory_space=pltpu.SMEM)
    dma = pltpu.SemaphoreType.DMA
    pm, lrows, sg, mg, bg = pl.pallas_call(
        kernel,
        out_shape=(
            jax.ShapeDtypeStruct((C, SLAB, W), BF),
            jax.ShapeDtypeStruct((C * SLAB, 128), BF),
            jax.ShapeDtypeStruct((8, 2, C, 2 * C), F32),
            jax.ShapeDtypeStruct((C, C), F32),
            jax.ShapeDtypeStruct((1, C), F32),
        ),
        in_specs=[hbm] * 9 + [vmem, smem],
        out_specs=(hbm, hbm, hbm, vmem, vmem),
        scratch_shapes=[
            pltpu.VMEM((C, SLAB, W), BF),
            pltpu.VMEM((C, SLAB, W), BF),
            pltpu.VMEM((C, SLAB, W), BF),
            pltpu.VMEM((C, SLAB, W), F32),
            pltpu.VMEM((2, 1024, 1024), BF),
            pltpu.VMEM((8, 2, C, 2 * C), BF),
            pltpu.VMEM((16, 128, 128), BF),
            pltpu.VMEM((W, 128), BF),
            pltpu.VMEM((W, 128), BF),
            pltpu.VMEM((128, W), BF),
            pltpu.VMEM((512, 256), BF),
            pltpu.VMEM((512, 128), BF),
            pltpu.VMEM((3, 256, 256), BF),
            pltpu.VMEM((SLAB, C, 128), F32),
            pltpu.VMEM((16, 128, 128), BF),
            pltpu.VMEM((SLAB, 64, 128), F32),
            pltpu.VMEM((C * SLAB, 128), BF),
            pltpu.VMEM((256, W), F32),
            pltpu.VMEM((256, W), F32),
            pltpu.VMEM((128, 128), BF),
            pltpu.VMEM((C, 128), F32),
            pltpu.VMEM((2, NZ, NQ, 64, 128), BF),
            pltpu.VMEM((2, NZ, NQ, 64, 128), BF),
            pltpu.VMEM((2, NZ, 128, 128), BF),
            pltpu.VMEM((2, NZ, 128, 128), BF),
            pltpu.VMEM((2, DP, 16, 128), BF),
            pltpu.VMEM((2, DP, 16, 128), BF),
            pltpu.VMEM((2, DP, 16, 128), BF),
            pltpu.VMEM((2, DP, 16, 128), BF),
            pltpu.VMEM((2, NZ, DP, 16, 128), BF),
            pltpu.VMEM((2, NZ, NQ, 64, 128), BF),
            pltpu.VMEM((2, NZ, NQ, 64, 128), BF),
            pltpu.VMEM((8, 2, C, 2 * C), F32),
            pltpu.VMEM((C, 1024), F32),
            pltpu.VMEM((NZ, 8, 128), F32),
            pltpu.VMEM((NZ, 8, 128), F32),
            pltpu.VMEM((DP, 8, 128), F32),
            pltpu.VMEM((NQ, 8, 128), F32),
            pltpu.VMEM((NZ, 8, 128), F32),
            pltpu.VMEM((3, 8, 128), F32),
            dma((16,)),
            dma((3,)),
            dma((2, NZ, NQ)), dma((2, NZ, NQ)),
            dma((2, NZ)), dma((2, NZ)),
            dma((2, DP)), dma((2, DP)),
            dma((2, DP)), dma((2, DP)),
            dma((2, NZ)), dma((2, NZ)),
            dma((2, NZ, NQ)), dma((2, NZ, NQ)),
            dma((4, 8)), dma((4, 8)),
        ],
        compiler_params=pltpu.CompilerParams(
            collective_id=0, has_side_effects=True, vmem_limit_bytes=58 * 1024 * 1024
        ),
        cost_estimate=pl.CostEstimate(
            flops=20_000_000_000, bytes_accessed=16_000_000, transcendentals=2_000_000
        ),
    )(field, cotangent, spectral_weight, colfwd, colinv_t, colinv, row_fwd, row_inv, perms,
      mixing_weight, bias)
    field_grad, spectral_grad, mixing_grad, bias_grad = pl.pallas_call(
        finish,
        out_shape=(
            jax.ShapeDtypeStruct((1, C, SLAB, W), BF),
            jax.ShapeDtypeStruct((8, 2, C, 2 * C), F32),
            jax.ShapeDtypeStruct((C, C), F32),
            jax.ShapeDtypeStruct((1, C), F32),
        ),
        in_specs=[hbm] * 4 + [vmem, vmem],
        out_specs=(hbm, hbm, vmem, vmem),
        scratch_shapes=[
            pltpu.VMEM((C, SLAB, W), BF),
            pltpu.VMEM((C * SLAB, 128), BF),
            pltpu.VMEM((128, W), BF),
            pltpu.VMEM((8, 2, C, 2 * C), F32),
            dma((11,)),
            dma((9,)),
        ],
        compiler_params=pltpu.CompilerParams(vmem_limit_bytes=58 * 1024 * 1024),
        cost_estimate=pl.CostEstimate(
            flops=600_000_000, bytes_accessed=10_000_000, transcendentals=0
        ),
    )(pm, lrows, colfwd_t, sg, mg, bg)
    return field_grad, spectral_grad, mixing_grad, bias_grad.reshape(C)


def solution(mesh):
    return jax.shard_map(
        per_device,
        mesh=mesh,
        in_specs=(
            P("dp", None, "space", None),
            P("dp", None, "space", None),
            P("dp", "space", None, None),
            P(),
            P(),
        ),
        out_specs=(P("dp", None, "space", None), P("dp", "space", None, None), P(), P()),
        check_vma=False,
    )
```

```python
import functools
import math

import jax
import jax.numpy as jnp
import ml_dtypes
import numpy as np
from jax import lax
from jax.experimental import pallas as pl
from jax.experimental.pallas import tpu as pltpu
from jax.sharding import PartitionSpec as P

C = 64
H = 1024
W = 1024
K1 = 64
K2 = 64
DP = 8
NZ = 8
NQ = 4
SLAB = 32
BF = jnp.bfloat16
F32 = jnp.float32
NN = (((1,), (0,)), ((), ()))
NT = (((1,), (1,)), ((), ()))


def build_tables():
    f32 = np.float32
    wpos = np.arange(W)[:, None]
    kpos = np.arange(K2)[None, :]
    angle = (wpos * kpos % W).astype(f32) * f32(2.0 * math.pi / W)
    scale = f32(1.0 / math.sqrt(W))
    cosine = np.cos(angle) * scale
    sine = np.sin(angle) * scale
    factor = np.where(kpos == 0, 1.0, 2.0).astype(f32)
    fwd = np.stack([cosine, -sine], 0).astype(ml_dtypes.bfloat16)
    inv = np.stack([factor * cosine, -factor * sine], 0).astype(ml_dtypes.bfloat16)
    z, xl, core, kk = np.meshgrid(
        np.arange(NZ), np.arange(2), np.arange(2), np.arange(2), indexing="ij"
    )
    order = (2 * (xl * 16 + z * 2 + core) + kk).reshape(-1)
    colfwd = fwd[:, :, order].transpose(1, 2, 0).reshape(W, 2 * K2)
    colinv_t = inv[:, :, order].transpose(1, 2, 0).reshape(W, 2 * K2)
    colinv = inv[:, :, order].transpose(0, 2, 1).reshape(2 * K2, W)
    colfwd_t = fwd[:, :, order].transpose(0, 2, 1).reshape(2 * K2, W)

    mpos = np.arange(K1)[:, None]
    freq = mpos + np.where(mpos >= K1 // 2, H - K1, 0)
    hpos = np.arange(H)[None, :]
    phase = (freq * hpos % H).astype(f32) * f32(2.0 * math.pi / H)
    rc = (np.cos(phase) / f32(math.sqrt(H))).astype(ml_dtypes.bfloat16)
    rs = (np.sin(phase) / f32(math.sqrt(H))).astype(ml_dtypes.bfloat16)
    fwd_rows = []
    inv_rows = []
    for zi in range(NZ):
        slabs = np.array([x * 16 + zi * 2 + c for x in range(2) for c in range(2)])
        rows = slabs[:, None, None] * SLAB + np.arange(16)[None, :, None] * 2 + np.arange(2)
        ct = rc[:, rows].reshape(DP, 8, NQ, 16, 2)
        st = rs[:, rows].reshape(DP, 8, NQ, 16, 2)
        big = np.zeros((2, 2, DP, 2, 8, NQ, 2, 2, 16), ml_dtypes.bfloat16)
        for hl in range(2):
            for k in range(2):
                big[hl, 0, :, k, :, :, k, 0] = ct[..., hl]
                big[hl, 0, :, k, :, :, k, 1] = st[..., hl]
                big[hl, 1, :, k, :, :, k, 0] = -st[..., hl]
                big[hl, 1, :, k, :, :, k, 1] = ct[..., hl]
        fwd_rows.append(big.reshape(512, 256))
        rows = slabs[:, None] * SLAB + np.arange(SLAB)[None, :]
        tab = np.zeros((2, NQ, 2, SLAB, DP, 2, 8), ml_dtypes.bfloat16)
        for i, t in enumerate((rc, rs)):
            v = t[:, rows].reshape(DP, 8, NQ, SLAB).transpose(2, 3, 0, 1)
            for k in range(2):
                tab[i, :, k, :, :, k, :] = v
        inv_rows.append(tab.reshape(512, 128))
    i = np.arange(256)
    sources = (
        32 * (i % 8) + i // 8,
        8 * (i % 32) + i // 32,
        16 * (i % 16) + i // 16,
    )
    perms = np.stack([np.eye(256)[s] for s in sources]).astype(ml_dtypes.bfloat16)
    return colfwd, colinv_t, colinv, colfwd_t, np.stack(fwd_rows), np.stack(inv_rows), perms


def far_first(i):
    step = (i + 1) // 2
    return lax.rem(4 + step * (2 * lax.rem(i, 2) - 1) + 8, 8)


def kernel(
    field_h, cot_h, sw_h, colfwd_h, colinvt_h, colinv_h, rowf_h, rowi_h, perm_h,
    mw, bias,
    pm_h, l_h, sg_h, mg_out, bg_out,
    field, cot, pgr, mix, kron, sw, wp, colfwd, colinvt, colinv, rowf, rowi,
    perm, slab, big, back, lrows, pre0, pre1, xkeep, strip, bcol,
    qs, qr, zs, zr, ds, dr, ms, mr, gr, us, ur, sg, mg, pack, prz, pdr, pqr, pgz, pk,
    in_sem, out_sem,
    s_ss, q_rs, z_rs, d_rs, m_rs, g_rs, u_rs, p_ss, p_rs,
):
    dp = lax.axis_index("dp")
    sp = lax.axis_index("space")
    z = lax.rem(sp // 2, NZ)
    q = (sp // 16) * 2 + lax.rem(sp, 2)

    def space_of(qq, zz):
        return (qq // 2) * 16 + zz * 2 + lax.rem(qq, 2)

    def quad_peer(r):
        qq = lax.rem(q + r, NQ)
        return qq, {"space": space_of(qq, z)}

    def z_peer(off):
        zz = lax.rem(z + off, NZ)
        return zz, {"space": space_of(q, zz)}

    def dp_peer(r):
        dd = lax.rem(dp + r, DP)
        return dd, {"dp": dd}

    def remote(src, dst, ss, rs, dev):
        return pltpu.make_async_remote_copy(
            src_ref=src, dst_ref=dst, send_sem=ss, recv_sem=rs,
            device_id=dev, device_id_type=pl.DeviceIdType.MESH,
        )

    def arrived(ref, sem):
        remote(ref, ref, sem, sem, quad_peer(1)[1]).wait_recv()

    def left(ref, sem):
        remote(ref, ref, sem, sem, quad_peer(1)[1]).wait_send()

    loads = [
        pltpu.make_async_copy(colfwd_h, colfwd, in_sem.at[0]),
        *[
            pltpu.make_async_copy(
                field_h.at[0, pl.ds(8 * i, 8)], field.at[pl.ds(8 * i, 8)], in_sem.at[1 + i]
            )
            for i in range(8)
        ],
        pltpu.make_async_copy(perm_h, perm, in_sem.at[15]),
        pltpu.make_async_copy(rowf_h.at[z], rowf, in_sem.at[9]),
        pltpu.make_async_copy(sw_h, sw, in_sem.at[10]),
        pltpu.make_async_copy(rowi_h.at[z], rowi, in_sem.at[11]),
        pltpu.make_async_copy(colinv_h, colinv, in_sem.at[12]),
        pltpu.make_async_copy(colinvt_h, colinvt, in_sem.at[13]),
        pltpu.make_async_copy(cot_h.at[0], cot, in_sem.at[14]),
    ]
    for copy in loads[:11]:
        copy.start()

    barrier = pltpu.get_barrier_semaphore()
    for r in range(1, NQ):
        pl.semaphore_signal(barrier, 1, device_id=quad_peer(r)[1], device_id_type=pl.DeviceIdType.MESH)
    for r in range(1, NZ):
        pl.semaphore_signal(barrier, 1, device_id=z_peer(r)[1], device_id_type=pl.DeviceIdType.MESH)
    for r in range(1, DP):
        pl.semaphore_signal(barrier, 1, device_id=dp_peer(r)[1], device_id_type=pl.DeviceIdType.MESH)

    low = lax.broadcasted_iota(jnp.int32, (64, 128), 1) < 64
    sign = jnp.where(low, -1.0, 1.0).astype(F32)
    low128 = lax.broadcasted_iota(jnp.int32, (128, 128), 1) < 64
    sign256 = jnp.where(lax.broadcasted_iota(jnp.int32, (256, 128), 1) < 64, -1.0, 1.0).astype(F32)

    def to_slab(blk, rows):
        res = lax.dot_general(perm[0], rows.astype(BF), NN, preferred_element_type=F32)
        slab[:, pl.ds(blk * 8 if isinstance(blk, int) else pl.multiple_of(blk * 8, 8), 8), :] = (
            res.reshape(SLAB, 8, 128)
        )

    def from_slab(blk):
        start = blk * 8 if isinstance(blk, int) else pl.multiple_of(blk * 8, 8)
        rows = slab[:, pl.ds(start, 8), :].reshape(256, 128).astype(BF)
        return lax.dot_general(perm[1], rows, NN, preferred_element_type=F32).astype(BF)

    def bias_rows(ch, carry):
        bcol[ch] = jnp.full((16, 128), bias[ch], F32)
        return carry

    lax.fori_loop(0, C, bias_rows, 0)

    loads[0].wait()
    loads[9].wait()
    for i in range(8):
        loads[1 + i].wait()
        rows = field[8 * i : 8 * i + 8].reshape(256, W)
        to_slab(i, lax.dot_general(rows, colfwd[...], NN, preferred_element_type=F32))
    for copy in loads[11:]:
        copy.start()
    pl.semaphore_wait(barrier, NQ + NZ + DP - 3)

    def build_kron(n, transposed):
        spread = (
            lax.broadcasted_iota(jnp.int32, (1024, 64), 0) // 16
            == lax.broadcasted_iota(jnp.int32, (1024, 64), 1)
        ).astype(F32).astype(BF)
        half = lax.dot_general(
            spread, mw[...], NT if transposed else NN, preferred_element_type=F32
        ).astype(BF)
        same = lax.rem(lax.broadcasted_iota(jnp.int32, (256, 1024), 0), 16) == lax.rem(
            lax.broadcasted_iota(jnp.int32, (256, 1024), 1), 16
        )
        for i in range(4):
            full = lax.dot_general(
                half[256 * i : 256 * i + 256], spread, NT, preferred_element_type=F32
            )
            kron[n, 256 * i : 256 * i + 256, :] = jnp.where(same, full, 0.0).astype(BF)

    def pointwise_tile(n, source, target, offset, i):
        hb = pl.multiple_of((i // 4) * 16, 16)
        wq = pl.multiple_of(lax.rem(i, 4) * 256, 256)
        rhs = source[:, pl.ds(hb, 16), pl.ds(wq, 256)].reshape(1024, 256)
        res = lax.dot_general(kron[n], rhs, NN, preferred_element_type=F32)
        res = res.reshape(64, 16, 256)
        if offset is not None:
            res = res + jnp.concatenate([offset[...], offset[...]], -1)
        target[:, pl.ds(hb, 16), pl.ds(wq, 256)] = res.astype(target.dtype)

    def some(tile, first, last):
        def one(i, carry):
            tile(i)
            return carry

        lax.fori_loop(first, last, one, 0)

    def mixgrad_tile(i):
        hb = pl.multiple_of((i // 4) * 16, 16)
        cb = pl.multiple_of(lax.rem(i, 4) * 16, 16)
        lhs = field[pl.ds(cb, 16), pl.ds(hb, 16), :].reshape(256, W)
        rhs = pgr[:, pl.ds(hb, 16), :].reshape(1024, W)
        res = lax.dot_general(lhs, rhs, NT, preferred_element_type=F32)
        same = lax.rem(lax.broadcasted_iota(jnp.int32, (256, 1024), 0), 16) == lax.rem(
            lax.broadcasted_iota(jnp.int32, (256, 1024), 1), 16
        )
        res = jnp.where(same, res, 0.0).reshape(16, 16, 1024).sum(1)
        mg[pl.ds(cb, 16), :] = mg[pl.ds(cb, 16), :] + res

    def quad_send(ph):
        for h2 in range(16):
            big[h2] = slab[2 * h2 : 2 * h2 + 2].reshape(128, 128).T.astype(BF)
        for zc in range(NZ):
            rows = big[:, zc * 16 : zc * 16 + 16, :].reshape(256, 128)
            res = lax.dot_general(perm[2], rows, NN, preferred_element_type=F32)
            qs[ph, zc] = res.astype(BF).reshape(NQ, 64, 128)

        def chunk(i, carry):
            zc = lax.rem(z + far_first(i), NZ)
            for r in range(1, NQ):
                qq, dev = quad_peer(r)
                remote(
                    qs.at[ph, zc, qq], qr.at[ph, zc, q], s_ss.at[0], q_rs.at[ph, zc], dev
                ).start()
            qr[ph, zc, q] = qs[ph, zc, q]
            return carry

        lax.fori_loop(0, NZ, chunk, 0)

    def quad_to_z(ph):
        def chunk(i, carry):
            zc = lax.rem(z + far_first(i), NZ)
            arrived(qr.at[ph, zc, pl.ds(0, 3)], q_rs.at[ph, zc])
            x = qr[ph, zc].reshape(256, 128)
            b = lax.dot_general(rowf[...], x, NN, preferred_element_type=F32)
            straight = jnp.where(low128, b[0:128], b[384:512])
            crossed = jnp.where(low128, b[128:256], b[256:384])
            zs[ph, zc] = (straight + pltpu.roll(crossed, 64, 1)).astype(BF)

            @pl.when(i < 7)
            def _():
                remote(
                    zs.at[ph, zc], zr.at[ph, z], s_ss.at[1], z_rs.at[ph],
                    {"space": space_of(q, zc)},
                ).start()

            return carry

        lax.fori_loop(0, NZ, chunk, 0)

    def z_sum(ph):
        total = zs[ph, z].astype(F32)
        arrived(zr.at[ph, pl.ds(0, 7)], z_rs.at[ph])
        for r in range(1, NZ):
            zz, dev = z_peer(r)
            total = total + zr[ph, zz].astype(F32)
        return total.astype(BF)

    def dp_out(ph, src, dst, ss, rs, value):
        src[ph] = value.reshape(DP, 16, 128)
        for r in range(1, DP):
            dd, dev = dp_peer(r)
            remote(src.at[ph, dd], dst.at[ph, dp], ss, rs.at[ph], dev).start()
        dst[ph, dp] = src[ph, dp]

    def dp_in(ph, dst, rs):
        arrived(dst.at[ph, pl.ds(0, 7)], rs.at[ph])
        return dst[ph].reshape(128, 128)

    row_mk = lax.rem(lax.broadcasted_iota(jnp.int32, (128, 128), 0), 16)
    col_mk = lax.rem(lax.broadcasted_iota(jnp.int32, (128, 128), 1), 16)

    def per_mode(x, dims):
        total = jnp.zeros((128, 128), F32)
        for mk in range(16):
            mine = jnp.where(row_mk == mk, x.astype(F32), 0.0).astype(BF)
            total = total + lax.dot_general(mine, wp[mk], dims, preferred_element_type=F32)
        return total.astype(BF)

    def z_send(ph):
        def one(i, carry):
            zz = lax.rem(z + far_first(i), NZ)
            remote(
                mr.at[ph], gr.at[ph, z], s_ss.at[4], g_rs.at[ph, z], {"space": space_of(q, zz)}
            ).start()
            return carry

        lax.fori_loop(0, 7, one, 0)
        gr[ph, z] = mr[ph]

    def z_to_quad(ph, early, between):
        def source(j, carry):
            j = jnp.int32(j)
            zc = lax.rem(z + far_first(7 - j), NZ)

            @pl.when(j > 0)
            def _():
                arrived(gr.at[ph, zc], g_rs.at[ph, zc])

            t = lax.dot_general(
                rowi[...], gr[ph, zc].reshape(128, 128), NN, preferred_element_type=F32
            )
            v = t[0:256] + pltpu.roll(t[256:512], 64, 1) * sign256
            us[ph, zc] = v.astype(BF).reshape(NQ, 64, 128)
            for r in range(1, NQ):
                qq, dev = quad_peer(r)
                remote(
                    us.at[ph, zc, qq], ur.at[ph, zc, q], s_ss.at[5], u_rs.at[ph, zc], dev
                ).start()
            ur[ph, zc, q] = us[ph, zc, q]
            return carry

        source(0, 0)
        early()
        lax.fori_loop(1, NZ, source, 0)
        between()

        def take(j, carry):
            zc = lax.rem(z + far_first(7 - j), NZ)
            arrived(ur.at[ph, zc, pl.ds(0, 3)], u_rs.at[ph, zc])
            res = lax.dot_general(
                perm[0], ur[ph, zc].reshape(256, 128), NN, preferred_element_type=F32
            )
            back[:, pl.ds(pl.multiple_of(zc * 8, 8), 8), :] = res.reshape(SLAB, 8, 128)
            return carry

        lax.fori_loop(0, NZ, take, 0)
        for h2 in range(16):
            t = back[2 * h2 : 2 * h2 + 2].reshape(128, 128).T
            re, im = t[0:64], t[64:128]
            slab[2 * h2] = jnp.where(low, re, pltpu.roll(im, 64, 1))
            slab[2 * h2 + 1] = jnp.where(low, pltpu.roll(re, 64, 1), im)

    field_mix = functools.partial(pointwise_tile, 0, field, mix, bcol)
    grad_mix = functools.partial(pointwise_tile, 1, pgr, cot, None)

    quad_send(0)
    build_kron(0, True)
    loads[10].wait()
    quad_to_z(0)
    some(field_mix, 0, 2)
    x = z_sum(0)
    dp_out(0, ds, dr, s_ss.at[2], d_rs, x)
    loads[11].wait()
    for m in range(8):
        for k in range(2):
            top = sw[m, k].astype(F32)
            bottom = pltpu.roll(top, 64, 1) * sign
            wp[k * 8 + m] = jnp.concatenate([top, bottom], 0).astype(BF)
    some(field_mix, 2, 5)
    mode_rows = dp_in(0, dr, d_rs)
    xkeep[...] = mode_rows
    dp_out(0, ms, mr, s_ss.at[3], m_rs, per_mode(mode_rows, NN))
    some(field_mix, 5, 8)
    mg[...] = jnp.zeros_like(mg)
    dp_in(0, mr, m_rs)
    z_send(0)
    loads[12].wait()

    def late_loads():
        for copy in loads[13:]:
            copy.wait()

    z_to_quad(0, functools.partial(build_kron, 1, False), late_loads)

    c1 = math.sqrt(2.0 / math.pi)
    c3 = c1 * 0.044715

    def pre_part(blk, pre):
        pre[...] = lax.dot_general(from_slab(blk), colinv[...], NN, preferred_element_type=F32)

    def slopes(blk, pre):
        for t in range(16):
            ch = blk * 8 + t // 2
            hh = slice(16 * (t % 2), 16 * (t % 2) + 16)
            v = pre[16 * t : 16 * t + 16, :] + mix[ch, hh, :]
            th = jnp.tanh((v * (c1 + c3 * (v * v))).astype(BF))
            vb = v.astype(BF)
            a = th * BF(0.5) + BF(0.5)
            rise = vb * (vb * vb * BF(6.0 * c3) + BF(2.0 * c1))
            slope = a + a * (BF(1.0) - a) * rise
            pgr[ch, hh, :] = cot[ch, hh, :] * slope

    def grad_part(blk):
        grads = pgr[pl.ds(pl.multiple_of(blk * 8, 8), 8)].reshape(256, W)
        rows = lax.dot_general(grads, colinvt[...], NN, preferred_element_type=F32)
        to_slab(blk, rows)
        strip[pl.ds(pl.multiple_of(blk * 8, 8), 8), :] = rows.reshape(8, SLAB, 128).sum(1)

    pre_part(0, pre0)

    def section(i, carry):
        blk = 2 * i
        pre_part(blk + 1, pre1)
        slopes(blk, pre0)
        grad_part(blk)
        pre_part(jnp.minimum(blk + 2, 6), pre0)
        slopes(blk + 1, pre1)
        grad_part(blk + 1)
        return carry

    lax.fori_loop(0, 4, section, 0)

    quad_send(1)
    quad_to_z(1)
    some(mixgrad_tile, 0, 3)
    g = z_sum(1)
    dp_out(1, ds, dr, s_ss.at[2], d_rs, g)
    some(mixgrad_tile, 3, 8)
    grad_rows = dp_in(1, dr, d_rs)
    dp_out(1, ms, mr, s_ss.at[3], m_rs, per_mode(grad_rows, NT))

    spread = (
        lax.broadcasted_iota(jnp.int32, (1024, 64), 0) // 16
        == lax.broadcasted_iota(jnp.int32, (1024, 64), 1)
    ).astype(F32).astype(BF)
    part = mg[...]
    hi = part.astype(BF)
    rest = part - hi.astype(F32)
    mid = rest.astype(BF)
    lo = (rest - mid.astype(F32)).astype(BF)
    part = (
        lax.dot_general(hi, spread, NN, preferred_element_type=F32)
        + lax.dot_general(mid, spread, NN, preferred_element_type=F32)
        + lax.dot_general(lo, spread, NN, preferred_element_type=F32)
    )
    bias_row = strip[...].T[0:1, :] * 32.0
    pack[...] = jnp.concatenate(
        [part, jnp.concatenate([bias_row, jnp.zeros((63, 64), F32)], 0)], 1
    ).reshape(NZ, 8, 128)
    for r in range(1, NZ):
        zz, dev = z_peer(r)
        remote(pack.at[zz], prz.at[z], p_ss.at[0], p_rs.at[0], dev).start()
    prz[z] = pack[z]

    some(grad_mix, 0, 4)

    arrived(prz.at[pl.ds(0, 7)], p_rs.at[0])
    pk[0] = prz[...].sum(0)
    for r in range(1, DP):
        dd, dev = dp_peer(r)
        remote(pk.at[0], pdr.at[dp], p_ss.at[1], p_rs.at[1], dev).start()
    pdr[dp] = pk[0]

    dp_in(1, mr, m_rs)
    z_send(1)

    pm_copy = pltpu.make_async_copy(cot, pm_h, out_sem.at[1])

    sg_copy = pltpu.make_async_copy(sg, sg_h, out_sem.at[0])

    def early():
        some(grad_mix, 4, 7)

        arrived(pdr.at[pl.ds(0, 7)], p_rs.at[1])
        pk[1] = pdr[...].sum(0)
        for r in range(1, NQ):
            qq, dev = quad_peer(r)
            remote(pk.at[1], pqr.at[q], p_ss.at[2], p_rs.at[2], dev).start()
        pqr[q] = pk[1]

    def totals():
        x_t = xkeep[...].astype(F32).T
        for m in range(8):
            for k in range(2):
                mine = jnp.where(col_mk == k * 8 + m, x_t, 0.0).astype(BF)
                prod = lax.dot_general(mine, grad_rows, NN, preferred_element_type=F32)
                sg[m, k] = prod[0:64] - pltpu.roll(prod[64:128], 64, 1) * sign
        sg_copy.start()
        some(grad_mix, 7, 8)
        pm_copy.start()
        arrived(pqr.at[pl.ds(0, 3)], p_rs.at[2])
        pk[2] = pqr[...].sum(0)
        for r in range(1, NZ):
            zz, dev = z_peer(r)
            remote(pk.at[2], pgz.at[z], p_ss.at[3], p_rs.at[3], dev).start()
        pgz[z] = pk[2]

    z_to_quad(1, early, totals)

    for blk in range(8):
        lrows[256 * blk : 256 * blk + 256, :] = from_slab(blk)
    l_copy = pltpu.make_async_copy(lrows, l_h, out_sem.at[2])
    l_copy.start()

    arrived(pgz.at[pl.ds(0, 7)], p_rs.at[3])
    norm = 1.0 / math.sqrt(DP * H * W)
    whole = pgz[...].reshape(64, 128) * norm
    mg_out[...] = whole[:, 0:64]
    bg_out[...] = whole[0:1, 64:128]

    left(qs.at[:, :, pl.ds(0, 3)], s_ss.at[0])
    left(zs.at[:, pl.ds(0, 7)], s_ss.at[1])
    left(ds.at[:, pl.ds(0, 7)], s_ss.at[2])
    left(ms.at[:, pl.ds(0, 7)], s_ss.at[3])
    left(gr.at[:, pl.ds(0, 7)], s_ss.at[4])
    left(us.at[:, :, pl.ds(0, 3)], s_ss.at[5])
    left(prz.at[pl.ds(0, 7)], p_ss.at[0])
    left(pdr.at[pl.ds(0, 7)], p_ss.at[1])
    left(pqr.at[pl.ds(0, 3)], p_ss.at[2])
    left(pgz.at[pl.ds(0, 7)], p_ss.at[3])
    sg_copy.wait()
    pm_copy.wait()
    l_copy.wait()


def finish(pm_h, l_h, colfwdt_h, sg_h, mg_in, bg_in, out_h, sg_out, mg_out, bg_out,
           pm, lrows, colfwdt, sg, in_sem, out_sem):
    loads = [
        pltpu.make_async_copy(l_h, lrows, in_sem.at[8]),
        pltpu.make_async_copy(colfwdt_h, colfwdt, in_sem.at[9]),
        *[
            pltpu.make_async_copy(pm_h.at[pl.ds(8 * i, 8)], pm.at[pl.ds(8 * i, 8)], in_sem.at[i])
            for i in range(8)
        ],
        pltpu.make_async_copy(sg_h, sg, in_sem.at[10]),
    ]
    for copy in loads:
        copy.start()
    mg_out[...] = mg_in[...]
    bg_out[...] = bg_in[...]
    loads[0].wait()
    loads[1].wait()
    stores = []
    for i in range(8):
        rows = lax.dot_general(
            lrows[256 * i : 256 * i + 256, :], colfwdt[...], NN, preferred_element_type=F32
        )
        loads[2 + i].wait()
        chs = slice(8 * i, 8 * i + 8)
        pm[chs] = (rows.reshape(8, SLAB, W) + pm[chs].astype(F32)).astype(BF)
        stores.append(pltpu.make_async_copy(pm.at[chs], out_h.at[0, chs], out_sem.at[i]))
        stores[-1].start()
    loads[10].wait()
    stores.append(pltpu.make_async_copy(sg, sg_out, out_sem.at[8]))
    stores[-1].start()
    for copy in stores:
        copy.wait()


def per_device(field, cotangent, spectral_weight, mixing_weight, bias):
    colfwd, colinv_t, colinv, colfwd_t, row_fwd, row_inv, perms = [
        jnp.asarray(t) for t in build_tables()
    ]
    hbm = pl.BlockSpec(memory_space=pl.ANY)
    vmem = pl.BlockSpec(memory_space=pltpu.VMEM)
    smem = pl.BlockSpec(memory_space=pltpu.SMEM)
    dma = pltpu.SemaphoreType.DMA
    pm, lrows, sg, mg, bg = pl.pallas_call(
        kernel,
        out_shape=(
            jax.ShapeDtypeStruct((C, SLAB, W), BF),
            jax.ShapeDtypeStruct((C * SLAB, 128), BF),
            jax.ShapeDtypeStruct((8, 2, C, 2 * C), F32),
            jax.ShapeDtypeStruct((C, C), F32),
            jax.ShapeDtypeStruct((1, C), F32),
        ),
        in_specs=[hbm] * 9 + [vmem, smem],
        out_specs=(hbm, hbm, hbm, vmem, vmem),
        scratch_shapes=[
            pltpu.VMEM((C, SLAB, W), BF),
            pltpu.VMEM((C, SLAB, W), BF),
            pltpu.VMEM((C, SLAB, W), BF),
            pltpu.VMEM((C, SLAB, W), F32),
            pltpu.VMEM((2, 1024, 1024), BF),
            pltpu.VMEM((8, 2, C, 2 * C), BF),
            pltpu.VMEM((16, 128, 128), BF),
            pltpu.VMEM((W, 128), BF),
            pltpu.VMEM((W, 128), BF),
            pltpu.VMEM((128, W), BF),
            pltpu.VMEM((512, 256), BF),
            pltpu.VMEM((512, 128), BF),
            pltpu.VMEM((3, 256, 256), BF),
            pltpu.VMEM((SLAB, C, 128), F32),
            pltpu.VMEM((16, 128, 128), BF),
            pltpu.VMEM((SLAB, 64, 128), F32),
            pltpu.VMEM((C * SLAB, 128), BF),
            pltpu.VMEM((256, W), F32),
            pltpu.VMEM((256, W), F32),
            pltpu.VMEM((128, 128), BF),
            pltpu.VMEM((C, 128), F32),
            pltpu.VMEM((C, 16, 128), F32),
            pltpu.VMEM((2, NZ, NQ, 64, 128), BF),
            pltpu.VMEM((2, NZ, NQ, 64, 128), BF),
            pltpu.VMEM((2, NZ, 128, 128), BF),
            pltpu.VMEM((2, NZ, 128, 128), BF),
            pltpu.VMEM((2, DP, 16, 128), BF),
            pltpu.VMEM((2, DP, 16, 128), BF),
            pltpu.VMEM((2, DP, 16, 128), BF),
            pltpu.VMEM((2, DP, 16, 128), BF),
            pltpu.VMEM((2, NZ, DP, 16, 128), BF),
            pltpu.VMEM((2, NZ, NQ, 64, 128), BF),
            pltpu.VMEM((2, NZ, NQ, 64, 128), BF),
            pltpu.VMEM((8, 2, C, 2 * C), F32),
            pltpu.VMEM((C, 1024), F32),
            pltpu.VMEM((NZ, 8, 128), F32),
            pltpu.VMEM((NZ, 8, 128), F32),
            pltpu.VMEM((DP, 8, 128), F32),
            pltpu.VMEM((NQ, 8, 128), F32),
            pltpu.VMEM((NZ, 8, 128), F32),
            pltpu.VMEM((3, 8, 128), F32),
            dma((16,)),
            dma((3,)),
            dma((6,)),
            dma((2, NZ)), dma((2,)), dma((2,)), dma((2,)), dma((2, NZ)), dma((2, NZ)),
            dma((4,)), dma((4,)),
        ],
        compiler_params=pltpu.CompilerParams(
            collective_id=0, has_side_effects=True, vmem_limit_bytes=58 * 1024 * 1024
        ),
        cost_estimate=pl.CostEstimate(
            flops=20_000_000_000, bytes_accessed=16_000_000, transcendentals=2_000_000
        ),
    )(field, cotangent, spectral_weight, colfwd, colinv_t, colinv, row_fwd, row_inv, perms,
      mixing_weight, bias)
    field_grad, spectral_grad, mixing_grad, bias_grad = pl.pallas_call(
        finish,
        out_shape=(
            jax.ShapeDtypeStruct((1, C, SLAB, W), BF),
            jax.ShapeDtypeStruct((8, 2, C, 2 * C), F32),
            jax.ShapeDtypeStruct((C, C), F32),
            jax.ShapeDtypeStruct((1, C), F32),
        ),
        in_specs=[hbm] * 4 + [vmem, vmem],
        out_specs=(hbm, hbm, vmem, vmem),
        scratch_shapes=[
            pltpu.VMEM((C, SLAB, W), BF),
            pltpu.VMEM((C * SLAB, 128), BF),
            pltpu.VMEM((128, W), BF),
            pltpu.VMEM((8, 2, C, 2 * C), F32),
            dma((11,)),
            dma((9,)),
        ],
        compiler_params=pltpu.CompilerParams(vmem_limit_bytes=58 * 1024 * 1024),
        cost_estimate=pl.CostEstimate(
            flops=600_000_000, bytes_accessed=10_000_000, transcendentals=0
        ),
    )(pm, lrows, colfwd_t, sg, mg, bg)
    return field_grad, spectral_grad, mixing_grad, bias_grad.reshape(C)


def solution(mesh):
    return jax.shard_map(
        per_device,
        mesh=mesh,
        in_specs=(
            P("dp", None, "space", None),
            P("dp", None, "space", None),
            P("dp", "space", None, None),
            P(),
            P(),
        ),
        out_specs=(P("dp", None, "space", None), P("dp", "space", None, None), P(), P()),
        check_vma=False,
    )
```

```python
import functools
import math

import jax
import jax.numpy as jnp
import ml_dtypes
import numpy as np
from jax import lax
from jax.experimental import pallas as pl
from jax.experimental.pallas import tpu as pltpu
from jax.sharding import PartitionSpec as P

C = 64
H = 1024
W = 1024
K1 = 64
K2 = 64
DP = 8
NZ = 8
NQ = 4
SLAB = 32
BF = jnp.bfloat16
F32 = jnp.float32
NN = (((1,), (0,)), ((), ()))
NT = (((1,), (1,)), ((), ()))


def build_tables():
    f32 = np.float32
    wpos = np.arange(W)[:, None]
    kpos = np.arange(K2)[None, :]
    angle = (wpos * kpos % W).astype(f32) * f32(2.0 * math.pi / W)
    scale = f32(1.0 / math.sqrt(W))
    cosine = np.cos(angle) * scale
    sine = np.sin(angle) * scale
    factor = np.where(kpos == 0, 1.0, 2.0).astype(f32)
    fwd = np.stack([cosine, -sine], 0).astype(ml_dtypes.bfloat16)
    inv = np.stack([factor * cosine, -factor * sine], 0).astype(ml_dtypes.bfloat16)
    z, xl, core, kk = np.meshgrid(
        np.arange(NZ), np.arange(2), np.arange(2), np.arange(2), indexing="ij"
    )
    order = (2 * (xl * 16 + z * 2 + core) + kk).reshape(-1)
    colfwd = fwd[:, :, order].transpose(1, 2, 0).reshape(W, 2 * K2)
    colinv_t = inv[:, :, order].transpose(1, 2, 0).reshape(W, 2 * K2)
    colinv = inv[:, :, order].transpose(0, 2, 1).reshape(2 * K2, W)
    colfwd_t = fwd[:, :, order].transpose(0, 2, 1).reshape(2 * K2, W)

    mpos = np.arange(K1)[:, None]
    freq = mpos + np.where(mpos >= K1 // 2, H - K1, 0)
    hpos = np.arange(H)[None, :]
    phase = (freq * hpos % H).astype(f32) * f32(2.0 * math.pi / H)
    rc = (np.cos(phase) / f32(math.sqrt(H))).astype(ml_dtypes.bfloat16)
    rs = (np.sin(phase) / f32(math.sqrt(H))).astype(ml_dtypes.bfloat16)
    fwd_rows = []
    inv_rows = []
    for zi in range(NZ):
        slabs = np.array([x * 16 + zi * 2 + c for x in range(2) for c in range(2)])
        rows = slabs[:, None, None] * SLAB + np.arange(16)[None, :, None] * 2 + np.arange(2)
        ct = rc[:, rows].reshape(DP, 8, NQ, 16, 2)
        st = rs[:, rows].reshape(DP, 8, NQ, 16, 2)
        big = np.zeros((2, 2, DP, 2, 8, NQ, 2, 2, 16), ml_dtypes.bfloat16)
        for hl in range(2):
            for k in range(2):
                big[hl, 0, :, k, :, :, k, 0] = ct[..., hl]
                big[hl, 0, :, k, :, :, k, 1] = st[..., hl]
                big[hl, 1, :, k, :, :, k, 0] = -st[..., hl]
                big[hl, 1, :, k, :, :, k, 1] = ct[..., hl]
        fwd_rows.append(big.reshape(512, 256))
        rows = slabs[:, None] * SLAB + np.arange(SLAB)[None, :]
        tab = np.zeros((2, NQ, 2, SLAB, DP, 2, 8), ml_dtypes.bfloat16)
        for i, t in enumerate((rc, rs)):
            v = t[:, rows].reshape(DP, 8, NQ, SLAB).transpose(2, 3, 0, 1)
            for k in range(2):
                tab[i, :, k, :, :, k, :] = v
        inv_rows.append(tab.reshape(512, 128))
    i = np.arange(256)
    sources = (
        32 * (i % 8) + i // 8,
        8 * (i % 32) + i // 32,
        16 * (i % 16) + i // 16,
    )
    perms = np.stack([np.eye(256)[s] for s in sources]).astype(ml_dtypes.bfloat16)
    return colfwd, colinv_t, colinv, colfwd_t, np.stack(fwd_rows), np.stack(inv_rows), perms


def far_first(i):
    step = (i + 1) // 2
    return lax.rem(4 + step * (2 * lax.rem(i, 2) - 1) + 8, 8)


def kernel(
    field_h, cot_h, sw_h, colfwd_h, colinvt_h, colinv_h, rowf_h, rowi_h, perm_h,
    mw, bias,
    pm_h, l_h, sg_h, mg_out, bg_out,
    field, cot, pgr, mix, kron, sw, wp, colfwd, colinvt, colinv, rowf, rowi,
    perm, slab, big, back, lrows, pre0, pre1, xkeep, strip, bcol,
    qs, qr, zs, zr, ds, dr, ms, mr, gr, us, ur, sg, mg, pack, prz, pdr, pqr, pgz, pk,
    in_sem, out_sem,
    s_ss, q_rs, z_rs, d_rs, m_rs, g_rs, u_rs, p_ss, p_rs,
):
    dp = lax.axis_index("dp")
    sp = lax.axis_index("space")
    z = lax.rem(sp // 2, NZ)
    q = (sp // 16) * 2 + lax.rem(sp, 2)

    def space_of(qq, zz):
        return (qq // 2) * 16 + zz * 2 + lax.rem(qq, 2)

    def quad_peer(r):
        qq = lax.rem(q + r, NQ)
        return qq, {"space": space_of(qq, z)}

    def z_peer(off):
        zz = lax.rem(z + off, NZ)
        return zz, {"space": space_of(q, zz)}

    def dp_peer(r):
        dd = lax.rem(dp + r, DP)
        return dd, {"dp": dd}

    def remote(src, dst, ss, rs, dev):
        return pltpu.make_async_remote_copy(
            src_ref=src, dst_ref=dst, send_sem=ss, recv_sem=rs,
            device_id=dev, device_id_type=pl.DeviceIdType.MESH,
        )

    def arrived(ref, sem):
        remote(ref, ref, sem, sem, quad_peer(1)[1]).wait_recv()

    def left(ref, sem):
        remote(ref, ref, sem, sem, quad_peer(1)[1]).wait_send()

    loads = [
        pltpu.make_async_copy(colfwd_h, colfwd, in_sem.at[0]),
        *[
            pltpu.make_async_copy(
                field_h.at[0, pl.ds(8 * i, 8)], field.at[pl.ds(8 * i, 8)], in_sem.at[1 + i]
            )
            for i in range(8)
        ],
        pltpu.make_async_copy(perm_h, perm, in_sem.at[15]),
        pltpu.make_async_copy(rowf_h.at[z], rowf, in_sem.at[9]),
        pltpu.make_async_copy(sw_h, sw, in_sem.at[10]),
        pltpu.make_async_copy(rowi_h.at[z], rowi, in_sem.at[11]),
        pltpu.make_async_copy(colinv_h, colinv, in_sem.at[12]),
        pltpu.make_async_copy(colinvt_h, colinvt, in_sem.at[13]),
        pltpu.make_async_copy(cot_h.at[0], cot, in_sem.at[14]),
    ]
    for copy in loads[:11]:
        copy.start()

    barrier = pltpu.get_barrier_semaphore()
    for r in range(1, NQ):
        pl.semaphore_signal(barrier, 1, device_id=quad_peer(r)[1], device_id_type=pl.DeviceIdType.MESH)
    for r in range(1, NZ):
        pl.semaphore_signal(barrier, 1, device_id=z_peer(r)[1], device_id_type=pl.DeviceIdType.MESH)
    for r in range(1, DP):
        pl.semaphore_signal(barrier, 1, device_id=dp_peer(r)[1], device_id_type=pl.DeviceIdType.MESH)

    low = lax.broadcasted_iota(jnp.int32, (64, 128), 1) < 64
    sign = jnp.where(low, -1.0, 1.0).astype(F32)
    low128 = lax.broadcasted_iota(jnp.int32, (128, 128), 1) < 64
    sign256 = jnp.where(lax.broadcasted_iota(jnp.int32, (256, 128), 1) < 64, -1.0, 1.0).astype(F32)

    def to_slab(blk, rows):
        res = lax.dot_general(perm[0], rows.astype(BF), NN, preferred_element_type=F32)
        slab[:, pl.ds(blk * 8 if isinstance(blk, int) else pl.multiple_of(blk * 8, 8), 8), :] = (
            res.reshape(SLAB, 8, 128)
        )

    def from_slab(blk):
        start = blk * 8 if isinstance(blk, int) else pl.multiple_of(blk * 8, 8)
        rows = slab[:, pl.ds(start, 8), :].reshape(256, 128).astype(BF)
        return lax.dot_general(perm[1], rows, NN, preferred_element_type=F32).astype(BF)

    def bias_rows(ch, carry):
        bcol[ch] = jnp.full((16, 128), bias[ch], F32)
        return carry

    lax.fori_loop(0, C, bias_rows, 0)

    loads[0].wait()
    loads[9].wait()
    for i in range(8):
        loads[1 + i].wait()
        rows = field[8 * i : 8 * i + 8].reshape(256, W)
        to_slab(i, lax.dot_general(rows, colfwd[...], NN, preferred_element_type=F32))
    for copy in loads[11:]:
        copy.start()
    pl.semaphore_wait(barrier, NQ + NZ + DP - 3)

    def build_kron(n, transposed):
        spread = (
            lax.broadcasted_iota(jnp.int32, (1024, 64), 0) // 16
            == lax.broadcasted_iota(jnp.int32, (1024, 64), 1)
        ).astype(F32).astype(BF)
        half = lax.dot_general(
            spread, mw[...], NT if transposed else NN, preferred_element_type=F32
        ).astype(BF)
        same = lax.rem(lax.broadcasted_iota(jnp.int32, (256, 1024), 0), 16) == lax.rem(
            lax.broadcasted_iota(jnp.int32, (256, 1024), 1), 16
        )
        for i in range(4):
            full = lax.dot_general(
                half[256 * i : 256 * i + 256], spread, NT, preferred_element_type=F32
            )
            kron[n, 256 * i : 256 * i + 256, :] = jnp.where(same, full, 0.0).astype(BF)

    def pointwise_tile(n, source, target, offset, i):
        hb = pl.multiple_of((i // 4) * 16, 16)
        wq = pl.multiple_of(lax.rem(i, 4) * 256, 256)
        rhs = source[:, pl.ds(hb, 16), pl.ds(wq, 256)].reshape(1024, 256)
        res = lax.dot_general(kron[n], rhs, NN, preferred_element_type=F32)
        res = res.reshape(64, 16, 256)
        if offset is not None:
            res = res + jnp.concatenate([offset[...], offset[...]], -1)
        target[:, pl.ds(hb, 16), pl.ds(wq, 256)] = res.astype(target.dtype)

    def some(tile, first, last):
        def one(i, carry):
            tile(i)
            return carry

        lax.fori_loop(first, last, one, 0)

    def mixgrad_tile(i):
        hb = pl.multiple_of((i // 4) * 16, 16)
        cb = pl.multiple_of(lax.rem(i, 4) * 16, 16)
        lhs = field[pl.ds(cb, 16), pl.ds(hb, 16), :].reshape(256, W)
        rhs = pgr[:, pl.ds(hb, 16), :].reshape(1024, W)
        res = lax.dot_general(lhs, rhs, NT, preferred_element_type=F32)
        same = lax.rem(lax.broadcasted_iota(jnp.int32, (256, 1024), 0), 16) == lax.rem(
            lax.broadcasted_iota(jnp.int32, (256, 1024), 1), 16
        )
        res = jnp.where(same, res, 0.0).reshape(16, 16, 1024).sum(1)
        mg[pl.ds(cb, 16), :] = mg[pl.ds(cb, 16), :] + res

    def quad_send(ph):
        for h2 in range(16):
            big[h2] = slab[2 * h2 : 2 * h2 + 2].reshape(128, 128).T.astype(BF)
        for zc in range(NZ):
            rows = big[:, zc * 16 : zc * 16 + 16, :].reshape(256, 128)
            res = lax.dot_general(perm[2], rows, NN, preferred_element_type=F32)
            qs[ph, zc] = res.astype(BF).reshape(NQ, 64, 128)

        def chunk(i, carry):
            zc = lax.rem(z + far_first(i), NZ)
            for r in range(1, NQ):
                qq, dev = quad_peer(r)
                remote(
                    qs.at[ph, zc, qq], qr.at[ph, zc, q], s_ss.at[0], q_rs.at[ph, zc], dev
                ).start()
            qr[ph, zc, q] = qs[ph, zc, q]
            return carry

        lax.fori_loop(0, NZ, chunk, 0)

    def quad_to_z(ph):
        def chunk(i, carry):
            zc = lax.rem(z + far_first(i), NZ)
            arrived(qr.at[ph, zc, pl.ds(0, 3)], q_rs.at[ph, zc])
            x = qr[ph, zc].reshape(256, 128)
            b = lax.dot_general(rowf[...], x, NN, preferred_element_type=F32)
            straight = jnp.where(low128, b[0:128], b[384:512])
            crossed = jnp.where(low128, b[128:256], b[256:384])
            zs[ph, zc] = (straight + pltpu.roll(crossed, 64, 1)).astype(BF)

            @pl.when(i < 7)
            def _():
                remote(
                    zs.at[ph, zc], zr.at[ph, z], s_ss.at[1], z_rs.at[ph],
                    {"space": space_of(q, zc)},
                ).start()

            return carry

        lax.fori_loop(0, NZ, chunk, 0)

    def z_sum(ph):
        total = zs[ph, z].astype(F32)
        arrived(zr.at[ph, pl.ds(0, 7)], z_rs.at[ph])
        for r in range(1, NZ):
            zz, dev = z_peer(r)
            total = total + zr[ph, zz].astype(F32)
        return total.astype(BF)

    def dp_out(ph, src, dst, ss, rs, value):
        src[ph] = value.reshape(DP, 16, 128)
        for r in range(1, DP):
            dd, dev = dp_peer(r)
            remote(src.at[ph, dd], dst.at[ph, dp], ss, rs.at[ph], dev).start()
        dst[ph, dp] = src[ph, dp]

    def dp_in(ph, dst, rs):
        arrived(dst.at[ph, pl.ds(0, 7)], rs.at[ph])
        return dst[ph].reshape(128, 128)

    row_mk = lax.rem(lax.broadcasted_iota(jnp.int32, (128, 128), 0), 16)
    col_mk = lax.rem(lax.broadcasted_iota(jnp.int32, (128, 128), 1), 16)

    def per_mode(x, dims):
        total = jnp.zeros((128, 128), F32)
        for mk in range(16):
            mine = jnp.where(row_mk == mk, x.astype(F32), 0.0).astype(BF)
            total = total + lax.dot_general(mine, wp[mk], dims, preferred_element_type=F32)
        return total.astype(BF)

    def z_send(ph):
        def one(i, carry):
            zz = lax.rem(z + far_first(i), NZ)
            remote(
                mr.at[ph], gr.at[ph, z], s_ss.at[4], g_rs.at[ph, z], {"space": space_of(q, zz)}
            ).start()
            return carry

        lax.fori_loop(0, 7, one, 0)
        gr[ph, z] = mr[ph]

    def z_to_quad(ph, early, between):
        def source(j, carry):
            j = jnp.int32(j)
            zc = lax.rem(z + far_first(7 - j), NZ)

            @pl.when(j > 0)
            def _():
                arrived(gr.at[ph, zc], g_rs.at[ph, zc])

            t = lax.dot_general(
                rowi[...], gr[ph, zc].reshape(128, 128), NN, preferred_element_type=F32
            )
            v = t[0:256] + pltpu.roll(t[256:512], 64, 1) * sign256
            us[ph, zc] = v.astype(BF).reshape(NQ, 64, 128)
            for r in range(1, NQ):
                qq, dev = quad_peer(r)
                remote(
                    us.at[ph, zc, qq], ur.at[ph, zc, q], s_ss.at[5], u_rs.at[ph, zc], dev
                ).start()
            ur[ph, zc, q] = us[ph, zc, q]
            return carry

        source(0, 0)
        early()
        lax.fori_loop(1, NZ, source, 0)
        between()

        def take(j, carry):
            zc = lax.rem(z + far_first(7 - j), NZ)
            arrived(ur.at[ph, zc, pl.ds(0, 3)], u_rs.at[ph, zc])
            res = lax.dot_general(
                perm[0], ur[ph, zc].reshape(256, 128), NN, preferred_element_type=F32
            )
            back[:, pl.ds(pl.multiple_of(zc * 8, 8), 8), :] = res.reshape(SLAB, 8, 128)
            return carry

        lax.fori_loop(0, NZ, take, 0)
        for h2 in range(16):
            t = back[2 * h2 : 2 * h2 + 2].reshape(128, 128).T
            re, im = t[0:64], t[64:128]
            slab[2 * h2] = jnp.where(low, re, pltpu.roll(im, 64, 1))
            slab[2 * h2 + 1] = jnp.where(low, pltpu.roll(re, 64, 1), im)

    field_mix = functools.partial(pointwise_tile, 0, field, mix, bcol)
    grad_mix = functools.partial(pointwise_tile, 1, pgr, cot, None)

    quad_send(0)
    build_kron(0, True)
    loads[10].wait()
    quad_to_z(0)
    some(field_mix, 0, 2)
    x = z_sum(0)
    dp_out(0, ds, dr, s_ss.at[2], d_rs, x)
    loads[11].wait()
    for m in range(8):
        for k in range(2):
            top = sw[m, k].astype(F32)
            bottom = pltpu.roll(top, 64, 1) * sign
            wp[k * 8 + m] = jnp.concatenate([top, bottom], 0).astype(BF)
    some(field_mix, 2, 5)
    mode_rows = dp_in(0, dr, d_rs)
    xkeep[...] = mode_rows
    dp_out(0, ms, mr, s_ss.at[3], m_rs, per_mode(mode_rows, NN))
    some(field_mix, 5, 8)
    mg[...] = jnp.zeros_like(mg)
    dp_in(0, mr, m_rs)
    z_send(0)
    loads[12].wait()

    def late_loads():
        for copy in loads[13:]:
            copy.wait()

    z_to_quad(0, functools.partial(build_kron, 1, False), late_loads)

    c1 = math.sqrt(2.0 / math.pi)
    c3 = c1 * 0.044715

    def pre_part(blk, pre):
        pre[...] = lax.dot_general(from_slab(blk), colinv[...], NN, preferred_element_type=F32)

    def slopes(blk, pre):
        for t in range(16):
            ch = blk * 8 + t // 2
            hh = slice(16 * (t % 2), 16 * (t % 2) + 16)
            v = pre[16 * t : 16 * t + 16, :] + mix[ch, hh, :]
            vb = v.astype(BF)
            v2 = vb * vb
            a = jnp.tanh(vb * (v2 * BF(c3) + BF(c1))) * BF(0.5) + BF(0.5)
            rise = vb * (v2 * BF(6.0 * c3) + BF(2.0 * c1))
            slope = a + a * (BF(1.0) - a) * rise
            pgr[ch, hh, :] = cot[ch, hh, :] * slope

    def grad_part(blk):
        grads = pgr[pl.ds(pl.multiple_of(blk * 8, 8), 8)].reshape(256, W)
        rows = lax.dot_general(grads, colinvt[...], NN, preferred_element_type=F32)
        to_slab(blk, rows)
        strip[pl.ds(pl.multiple_of(blk * 8, 8), 8), :] = rows.reshape(8, SLAB, 128).sum(1)

    pre_part(0, pre0)

    def section(i, carry):
        blk = 2 * i
        pre_part(blk + 1, pre1)
        slopes(blk, pre0)
        grad_part(blk)
        pre_part(jnp.minimum(blk + 2, 6), pre0)
        slopes(blk + 1, pre1)
        grad_part(blk + 1)
        return carry

    lax.fori_loop(0, 4, section, 0)

    quad_send(1)
    quad_to_z(1)
    some(mixgrad_tile, 0, 3)
    g = z_sum(1)
    dp_out(1, ds, dr, s_ss.at[2], d_rs, g)
    some(mixgrad_tile, 3, 8)
    grad_rows = dp_in(1, dr, d_rs)
    dp_out(1, ms, mr, s_ss.at[3], m_rs, per_mode(grad_rows, NT))

    spread = (
        lax.broadcasted_iota(jnp.int32, (1024, 64), 0) // 16
        == lax.broadcasted_iota(jnp.int32, (1024, 64), 1)
    ).astype(F32).astype(BF)
    part = mg[...]
    hi = part.astype(BF)
    rest = part - hi.astype(F32)
    mid = rest.astype(BF)
    lo = (rest - mid.astype(F32)).astype(BF)
    part = (
        lax.dot_general(hi, spread, NN, preferred_element_type=F32)
        + lax.dot_general(mid, spread, NN, preferred_element_type=F32)
        + lax.dot_general(lo, spread, NN, preferred_element_type=F32)
    )
    bias_row = strip[...].T[0:1, :] * 32.0
    pack[...] = jnp.concatenate(
        [part, jnp.concatenate([bias_row, jnp.zeros((63, 64), F32)], 0)], 1
    ).reshape(NZ, 8, 128)
    for r in range(1, NZ):
        zz, dev = z_peer(r)
        remote(pack.at[zz], prz.at[z], p_ss.at[0], p_rs.at[0], dev).start()
    prz[z] = pack[z]

    some(grad_mix, 0, 4)

    arrived(prz.at[pl.ds(0, 7)], p_rs.at[0])
    pk[0] = prz[...].sum(0)
    for r in range(1, DP):
        dd, dev = dp_peer(r)
        remote(pk.at[0], pdr.at[dp], p_ss.at[1], p_rs.at[1], dev).start()
    pdr[dp] = pk[0]

    dp_in(1, mr, m_rs)
    z_send(1)

    pm_copy = pltpu.make_async_copy(cot, pm_h, out_sem.at[1])

    sg_copy = pltpu.make_async_copy(sg, sg_h, out_sem.at[0])

    def early():
        some(grad_mix, 4, 7)

        arrived(pdr.at[pl.ds(0, 7)], p_rs.at[1])
        pk[1] = pdr[...].sum(0)
        for r in range(1, NQ):
            qq, dev = quad_peer(r)
            remote(pk.at[1], pqr.at[q], p_ss.at[2], p_rs.at[2], dev).start()
        pqr[q] = pk[1]

    def totals():
        x_t = xkeep[...].astype(F32).T
        for m in range(8):
            for k in range(2):
                mine = jnp.where(col_mk == k * 8 + m, x_t, 0.0).astype(BF)
                prod = lax.dot_general(mine, grad_rows, NN, preferred_element_type=F32)
                sg[m, k] = prod[0:64] - pltpu.roll(prod[64:128], 64, 1) * sign
        sg_copy.start()
        some(grad_mix, 7, 8)
        pm_copy.start()
        arrived(pqr.at[pl.ds(0, 3)], p_rs.at[2])
        pk[2] = pqr[...].sum(0)
        for r in range(1, NZ):
            zz, dev = z_peer(r)
            remote(pk.at[2], pgz.at[z], p_ss.at[3], p_rs.at[3], dev).start()
        pgz[z] = pk[2]

    z_to_quad(1, early, totals)

    for blk in range(8):
        lrows[256 * blk : 256 * blk + 256, :] = from_slab(blk)
    l_copy = pltpu.make_async_copy(lrows, l_h, out_sem.at[2])
    l_copy.start()

    arrived(pgz.at[pl.ds(0, 7)], p_rs.at[3])
    norm = 1.0 / math.sqrt(DP * H * W)
    whole = pgz[...].reshape(64, 128) * norm
    mg_out[...] = whole[:, 0:64]
    bg_out[...] = whole[0:1, 64:128]

    left(qs.at[:, :, pl.ds(0, 3)], s_ss.at[0])
    left(zs.at[:, pl.ds(0, 7)], s_ss.at[1])
    left(ds.at[:, pl.ds(0, 7)], s_ss.at[2])
    left(ms.at[:, pl.ds(0, 7)], s_ss.at[3])
    left(gr.at[:, pl.ds(0, 7)], s_ss.at[4])
    left(us.at[:, :, pl.ds(0, 3)], s_ss.at[5])
    left(prz.at[pl.ds(0, 7)], p_ss.at[0])
    left(pdr.at[pl.ds(0, 7)], p_ss.at[1])
    left(pqr.at[pl.ds(0, 3)], p_ss.at[2])
    left(pgz.at[pl.ds(0, 7)], p_ss.at[3])
    sg_copy.wait()
    pm_copy.wait()
    l_copy.wait()


def finish(pm_h, l_h, colfwdt_h, sg_h, mg_in, bg_in, out_h, sg_out, mg_out, bg_out,
           pm, lrows, colfwdt, sg, in_sem, out_sem):
    loads = [
        pltpu.make_async_copy(l_h, lrows, in_sem.at[8]),
        pltpu.make_async_copy(colfwdt_h, colfwdt, in_sem.at[9]),
        *[
            pltpu.make_async_copy(pm_h.at[pl.ds(8 * i, 8)], pm.at[pl.ds(8 * i, 8)], in_sem.at[i])
            for i in range(8)
        ],
        pltpu.make_async_copy(sg_h, sg, in_sem.at[10]),
    ]
    for copy in loads:
        copy.start()
    mg_out[...] = mg_in[...]
    bg_out[...] = bg_in[...]
    loads[0].wait()
    loads[1].wait()
    stores = []
    for i in range(8):
        rows = lax.dot_general(
            lrows[256 * i : 256 * i + 256, :], colfwdt[...], NN, preferred_element_type=F32
        )
        loads[2 + i].wait()
        chs = slice(8 * i, 8 * i + 8)
        pm[chs] = (rows.reshape(8, SLAB, W) + pm[chs].astype(F32)).astype(BF)
        stores.append(pltpu.make_async_copy(pm.at[chs], out_h.at[0, chs], out_sem.at[i]))
        stores[-1].start()
    loads[10].wait()
    stores.append(pltpu.make_async_copy(sg, sg_out, out_sem.at[8]))
    stores[-1].start()
    for copy in stores:
        copy.wait()


def per_device(field, cotangent, spectral_weight, mixing_weight, bias):
    colfwd, colinv_t, colinv, colfwd_t, row_fwd, row_inv, perms = [
        jnp.asarray(t) for t in build_tables()
    ]
    hbm = pl.BlockSpec(memory_space=pl.ANY)
    vmem = pl.BlockSpec(memory_space=pltpu.VMEM)
    smem = pl.BlockSpec(memory_space=pltpu.SMEM)
    dma = pltpu.SemaphoreType.DMA
    pm, lrows, sg, mg, bg = pl.pallas_call(
        kernel,
        out_shape=(
            jax.ShapeDtypeStruct((C, SLAB, W), BF),
            jax.ShapeDtypeStruct((C * SLAB, 128), BF),
            jax.ShapeDtypeStruct((8, 2, C, 2 * C), F32),
            jax.ShapeDtypeStruct((C, C), F32),
            jax.ShapeDtypeStruct((1, C), F32),
        ),
        in_specs=[hbm] * 9 + [vmem, smem],
        out_specs=(hbm, hbm, hbm, vmem, vmem),
        scratch_shapes=[
            pltpu.VMEM((C, SLAB, W), BF),
            pltpu.VMEM((C, SLAB, W), BF),
            pltpu.VMEM((C, SLAB, W), BF),
            pltpu.VMEM((C, SLAB, W), F32),
            pltpu.VMEM((2, 1024, 1024), BF),
            pltpu.VMEM((8, 2, C, 2 * C), BF),
            pltpu.VMEM((16, 128, 128), BF),
            pltpu.VMEM((W, 128), BF),
            pltpu.VMEM((W, 128), BF),
            pltpu.VMEM((128, W), BF),
            pltpu.VMEM((512, 256), BF),
            pltpu.VMEM((512, 128), BF),
            pltpu.VMEM((3, 256, 256), BF),
            pltpu.VMEM((SLAB, C, 128), F32),
            pltpu.VMEM((16, 128, 128), BF),
            pltpu.VMEM((SLAB, 64, 128), F32),
            pltpu.VMEM((C * SLAB, 128), BF),
            pltpu.VMEM((256, W), F32),
            pltpu.VMEM((256, W), F32),
            pltpu.VMEM((128, 128), BF),
            pltpu.VMEM((C, 128), F32),
            pltpu.VMEM((C, 16, 128), F32),
            pltpu.VMEM((2, NZ, NQ, 64, 128), BF),
            pltpu.VMEM((2, NZ, NQ, 64, 128), BF),
            pltpu.VMEM((2, NZ, 128, 128), BF),
            pltpu.VMEM((2, NZ, 128, 128), BF),
            pltpu.VMEM((2, DP, 16, 128), BF),
            pltpu.VMEM((2, DP, 16, 128), BF),
            pltpu.VMEM((2, DP, 16, 128), BF),
            pltpu.VMEM((2, DP, 16, 128), BF),
            pltpu.VMEM((2, NZ, DP, 16, 128), BF),
            pltpu.VMEM((2, NZ, NQ, 64, 128), BF),
            pltpu.VMEM((2, NZ, NQ, 64, 128), BF),
            pltpu.VMEM((8, 2, C, 2 * C), F32),
            pltpu.VMEM((C, 1024), F32),
            pltpu.VMEM((NZ, 8, 128), F32),
            pltpu.VMEM((NZ, 8, 128), F32),
            pltpu.VMEM((DP, 8, 128), F32),
            pltpu.VMEM((NQ, 8, 128), F32),
            pltpu.VMEM((NZ, 8, 128), F32),
            pltpu.VMEM((3, 8, 128), F32),
            dma((16,)),
            dma((3,)),
            dma((6,)),
            dma((2, NZ)), dma((2,)), dma((2,)), dma((2,)), dma((2, NZ)), dma((2, NZ)),
            dma((4,)), dma((4,)),
        ],
        compiler_params=pltpu.CompilerParams(
            collective_id=0, has_side_effects=True, vmem_limit_bytes=58 * 1024 * 1024
        ),
        cost_estimate=pl.CostEstimate(
            flops=20_000_000_000, bytes_accessed=16_000_000, transcendentals=2_000_000
        ),
    )(field, cotangent, spectral_weight, colfwd, colinv_t, colinv, row_fwd, row_inv, perms,
      mixing_weight, bias)
    field_grad, spectral_grad, mixing_grad, bias_grad = pl.pallas_call(
        finish,
        out_shape=(
            jax.ShapeDtypeStruct((1, C, SLAB, W), BF),
            jax.ShapeDtypeStruct((8, 2, C, 2 * C), F32),
            jax.ShapeDtypeStruct((C, C), F32),
            jax.ShapeDtypeStruct((1, C), F32),
        ),
        in_specs=[hbm] * 4 + [vmem, vmem],
        out_specs=(hbm, hbm, vmem, vmem),
        scratch_shapes=[
            pltpu.VMEM((C, SLAB, W), BF),
            pltpu.VMEM((C * SLAB, 128), BF),
            pltpu.VMEM((128, W), BF),
            pltpu.VMEM((8, 2, C, 2 * C), F32),
            dma((11,)),
            dma((9,)),
        ],
        compiler_params=pltpu.CompilerParams(vmem_limit_bytes=58 * 1024 * 1024),
        cost_estimate=pl.CostEstimate(
            flops=600_000_000, bytes_accessed=10_000_000, transcendentals=0
        ),
    )(pm, lrows, colfwd_t, sg, mg, bg)
    return field_grad, spectral_grad, mixing_grad, bias_grad.reshape(C)


def solution(mesh):
    return jax.shard_map(
        per_device,
        mesh=mesh,
        in_specs=(
            P("dp", None, "space", None),
            P("dp", None, "space", None),
            P("dp", "space", None, None),
            P(),
            P(),
        ),
        out_specs=(P("dp", None, "space", None), P("dp", "space", None, None), P(), P()),
        check_vma=False,
    )
```
